32 devices in a mesh: region: 16 (over z, y, x), band: 2 (over core).
Axes of the slice: x: 2, y: 2, z: 4, core: 2. Of those that a mesh axis runs over, the one named last changes fastest.
Arguments:
- emission: bfloat16 [16384, 192], P(('region', 'band')), may hold values from 0.099609375 to 10
- path_sends: int32 [32, 32, 64], P(('region', 'band')), may hold values from -1 to 511, as said below
- tile_slots: int32 [256, 512], P(('region', 'band')), may hold values from -1 to 2047, as said below
- geometry: bfloat16 [256, 256, 512], P(('region', 'band')), may hold values from 0.00049972534 to 0.0099487305
- absorption: bfloat16 [256, 8, 512], P(('region', 'band')), may hold values from 0.099609375 to 1
- hour_period: int32 [24], replicated, may hold values from 0 to 2
- dwellings: int32 [65536], P(('region', 'band')), may hold values from 1 to 8
- addr_sends: int32 [32, 32, 16], P(('region', 'band')), may hold values from -1 to 2047, as said below
- addr_building: int32 [32, 32, 16], P(('region', 'band')), may hold values from 0 to 2047
Outputs:
- receiver_level: float32 [65536], P(('region', 'band'))
- building_level: float32 [65536], P(('region', 'band'))
- exposure: float32 [65536, 192], P(('region', 'band'))
The draws below stay inside these ranges and needn't reach their ends.
Inputs may be any that keep to these rules, and one draw needn't show every extreme that they name: path_sends[s, d, c] is a segment of device s or -1; the live entries of each list come first; some destination gets 64 live entries from every source. tile_slots[t, p] names a received slot s * 64 + c of the tile's device whose entry path_sends[s, d, c] is live, or is -1; live entries of a tile come first, at least 256 of them, and some tile of every device has all 512 live; a slot may feed several paths. addr_sends[s, d, c] is a receiver of device s or -1; live entries of each list come first; each receiver is named at most once over all lists; some destination gets 16 live entries from every source.
All inputs are finite; a program needn't handle non-finite values.
Results may differ from the reference program's by a relative error of at most 0.00034.
Values may be sent and summed in bfloat16 or wider, within the bound.
No kernel may reach another device: no remote copies, remote signals or barrier semaphores. Data moves between devices by JAX's collectives and lax.ppermute only.
A program may use at most 64 MiB of HBM per device.

```python
import math
import jax
import jax.numpy as jnp
from jax import lax

BANDS = 8
HOURS = 24
SEG_DEV = 512
CAP = 64
TILE_DEV = 8
RECV_TILE = 256
PATHS_TILE = 512
CAP_ADDR = 16
BLD_DEV = 2048
SEGS = 16384
TILES = 256
RECV_DEV = 2048
RECV = 65536
BLDS = 65536
DEVICES = 32


def path_tables(key):
    keys = jax.random.split(jax.random.fold_in(key, 11), 7)
    counts = jax.random.randint(keys[0], (DEVICES, DEVICES), 1, CAP + 1, dtype=jnp.int32)
    full_dest = jax.random.randint(keys[1], (), 0, DEVICES, dtype=jnp.int32)
    counts = jnp.where(jnp.arange(DEVICES)[None, :] == full_dest, CAP, counts)
    chosen = jax.random.randint(keys[2], (DEVICES, DEVICES, CAP), 0, SEG_DEV, dtype=jnp.int32)
    send_list = jnp.where(jnp.arange(CAP)[None, None, :] < counts[:, :, None], chosen, -1)
    source = jax.random.randint(keys[3], (DEVICES, TILE_DEV * PATHS_TILE), 0, DEVICES, dtype=jnp.int32)
    live_count = jnp.take_along_axis(counts.T, source, axis=1)
    slot_pick = jax.random.randint(keys[4], source.shape, 0, 1 << 20, dtype=jnp.int32) % live_count
    picked = (source * CAP + slot_pick).reshape(DEVICES, TILE_DEV, PATHS_TILE)
    lengths = jax.random.randint(keys[5], (DEVICES, TILE_DEV), PATHS_TILE // 2, PATHS_TILE + 1, dtype=jnp.int32)
    full_tile = jax.random.randint(keys[6], (DEVICES, 1), 0, TILE_DEV, dtype=jnp.int32)
    lengths = jnp.where(jnp.arange(TILE_DEV)[None, :] == full_tile, PATHS_TILE, lengths)
    slot_table = jnp.where(jnp.arange(PATHS_TILE)[None, None, :] < lengths[:, :, None], picked, -1)
    return (send_list.astype(jnp.int32), slot_table.reshape(DEVICES * TILE_DEV, PATHS_TILE).astype(jnp.int32))


def draw_path_sends(key, part):
    return path_tables(key)[0]


def draw_tile_slots(key, part):
    return path_tables(key)[1]


def draw_addr_sends(key, part):
    keys = jax.random.split(jax.random.fold_in(key, 23), 3)
    counts = jax.random.randint(keys[0], (DEVICES, DEVICES), 1, CAP_ADDR + 1, dtype=jnp.int32)
    full_dest = jax.random.randint(keys[1], (), 0, DEVICES, dtype=jnp.int32)
    counts = jnp.where(jnp.arange(DEVICES)[None, :] == full_dest, CAP_ADDR, counts)
    rolled = jnp.roll(counts, -full_dest, axis=1)
    starts = jnp.roll(jnp.cumsum(rolled, axis=1) - rolled, full_dest, axis=1)
    orders = jax.vmap(lambda subkey: jax.random.permutation(subkey, RECV_DEV))(jax.random.split(keys[2], DEVICES))
    position = starts[:, :, None] + jnp.arange(CAP_ADDR)[None, None, :]
    is_live = (jnp.arange(CAP_ADDR)[None, None, :] < counts[:, :, None]) & (position < RECV_DEV)
    named = jnp.take_along_axis(orders, jnp.minimum(position, RECV_DEV - 1).reshape(DEVICES, -1), axis=1)
    named = named.reshape(DEVICES, DEVICES, CAP_ADDR)
    return jnp.where(is_live, named, -1).astype(jnp.int32)


def touch_ends(drawn, own_key, low, high):
    extent = drawn.shape
    index_at = [jax.random.randint(jax.random.fold_in(own_key, axis), (), 0, extent[axis]) for axis in range(len(extent))]
    drawn = drawn.at[tuple(index_at)].set(low)
    longest = extent.index(max(extent))
    index_at[longest] = (index_at[longest] + 1) % extent[longest]
    return drawn.at[tuple(index_at)].set(high)


def block_scale(rng, extent, cuts, low, top_value):
    level, own = 1.0, jax.random.fold_in(rng, 6)
    for dim, blocks in cuts:
        heights = jnp.exp(jax.random.uniform(jax.random.fold_in(own, dim), (blocks,), jnp.float32, low / len(cuts), top_value / len(cuts)))
        level = level * jnp.repeat(heights, extent[dim] // blocks).reshape([-1 if axis == dim else 1 for axis in range(len(extent))])
    return level


def setup_inputs(seed: int = 0) -> dict:
    splits = jax.random.split(jax.random.key(seed), 10)
    emission = jnp.clip(jnp.exp(math.log(10.0) - 4.609084 * jax.random.uniform(splits[0], (SEGS, BANDS * HOURS), jnp.float32) ** block_scale(splits[0], (SEGS, BANDS * HOURS), ((0, 32),), -0.2, 0.2)), 0.099609375, 10.0).astype(jnp.bfloat16)
    path_sends = draw_path_sends(jax.random.fold_in(splits[9], 71), 0)
    tile_slots = draw_tile_slots(jax.random.fold_in(splits[9], 71), 0)
    geometry = jnp.clip(jnp.exp(math.log(0.0099487305) - 2.9911416 * jax.random.uniform(splits[3], (TILES, RECV_TILE, PATHS_TILE), jnp.float32) ** block_scale(splits[3], (TILES, RECV_TILE, PATHS_TILE), ((0, 32),), -0.2, 0.2)), 0.00049972534, 0.0099487305).astype(jnp.bfloat16)
    absorption = jnp.clip(jnp.exp(math.log(1.0) - 2.306499 * jax.random.uniform(splits[4], (TILES, BANDS, PATHS_TILE), jnp.float32) ** block_scale(splits[4], (TILES, BANDS, PATHS_TILE), ((0, 32),), -0.2, 0.2)), 0.099609375, 1.0).astype(jnp.bfloat16)
    hour_period = touch_ends(jax.random.randint(splits[5], (HOURS,), 0, 3), jax.random.fold_in(splits[5], 1), 0, 2).astype(jnp.int32)
    dwellings = touch_ends(jax.random.randint(splits[6], (RECV,), 1, 9), jax.random.fold_in(splits[6], 1), 1, 8).astype(jnp.int32)
    addr_sends = draw_addr_sends(jax.random.fold_in(splits[9], 71), 0)
    addr_building = touch_ends(jax.random.randint(splits[8], (DEVICES, DEVICES, CAP_ADDR), 0, BLD_DEV), jax.random.fold_in(splits[8], 1), 0, BLD_DEV - 1).astype(jnp.int32)
    return {"emission": emission, "path_sends": path_sends, "tile_slots": tile_slots, "geometry": geometry, "absorption": absorption, "hour_period": hour_period, "dwellings": dwellings, "addr_sends": addr_sends, "addr_building": addr_building}


A_WEIGHTING_DB = [-26.2, -16.1, -8.6, -3.2, 0.0, 1.2, 1.0, -1.1]


def hour_weights(hour_period):
    a_weight = jnp.power(10.0, jnp.array(A_WEIGHTING_DB, jnp.float32) / 10.0)
    period_gain = jnp.array([1.0, 10.0 ** 0.5, 10.0], jnp.float32)
    matches = hour_period[:, None] == jnp.arange(3, dtype=jnp.int32)[None, :]
    per_hour = jnp.sum(jnp.where(matches, period_gain[None, :], jnp.float32(0.0)), axis=1)
    return (a_weight[:, None] * per_hour[None, :] / HOURS).reshape(-1)


def device_levels(emission, weights, items):
    send_column, slot_table, geometry, absorption = items
    row_index = jnp.arange(DEVICES, dtype=jnp.int32)[:, None] * SEG_DEV + jnp.maximum(send_column, 0)
    arrived = jnp.where(send_column[:, :, None] >= 0, emission[row_index], jnp.zeros((), jnp.bfloat16))
    arrived = arrived.reshape(DEVICES * CAP, BANDS * HOURS)
    gathered = jnp.where(slot_table[:, :, None] >= 0, arrived[jnp.maximum(slot_table, 0)], jnp.zeros((), jnp.bfloat16))
    factor = jnp.repeat(jnp.swapaxes(absorption, 1, 2), HOURS, axis=2)
    mixed_rows = (factor.astype(jnp.float32) * gathered.astype(jnp.float32)).astype(jnp.bfloat16)
    exposure = jnp.einsum("trp,tpc->trc", geometry.astype(jnp.float32), mixed_rows.astype(jnp.float32))
    flat_rows = exposure.reshape(-1, BANDS * HOURS)
    energy = jnp.dot(flat_rows, weights, precision=lax.Precision.HIGHEST)
    return jnp.log10(energy), flat_rows


def reference(emission, path_sends, tile_slots, geometry, absorption, hour_period, dwellings, addr_sends, addr_building):
    weights = hour_weights(hour_period)
    items = (jnp.swapaxes(path_sends, 0, 1),
             tile_slots.reshape(DEVICES, TILE_DEV, PATHS_TILE),
             geometry.reshape(DEVICES, TILE_DEV, RECV_TILE, PATHS_TILE),
             absorption.reshape(DEVICES, TILE_DEV, BANDS, PATHS_TILE))
    levels, exposure = lax.map(lambda piece: device_levels(emission, weights, piece), items)
    safe_index = jnp.maximum(addr_sends, 0).reshape(DEVICES, -1)
    is_live = addr_sends >= 0
    level_at = jnp.take_along_axis(levels, safe_index, axis=1).reshape(addr_sends.shape)
    dwell_all = dwellings.reshape(DEVICES, RECV_DEV).astype(jnp.float32)
    dwell_at = jnp.take_along_axis(dwell_all, safe_index, axis=1).reshape(addr_sends.shape)
    dwelt = jnp.where(is_live, dwell_at, jnp.float32(0.0))
    weighted = jnp.where(is_live, dwell_at * level_at, jnp.float32(0.0))
    dwelt = jnp.swapaxes(dwelt, 0, 1)
    weighted = jnp.swapaxes(weighted, 0, 1)
    segment_ids = jnp.arange(DEVICES, dtype=jnp.int32)[:, None, None] * BLD_DEV + addr_building
    numer = jax.ops.segment_sum(weighted.reshape(-1), segment_ids.reshape(-1), num_segments=BLDS)
    denom = jax.ops.segment_sum(dwelt.reshape(-1), segment_ids.reshape(-1), num_segments=BLDS)
    building_level = numer / jnp.maximum(denom, jnp.float32(1.0))
    return levels.reshape(-1), building_level, exposure.reshape(-1, BANDS * HOURS)
```

```python
import functools

import jax
import jax.numpy as jnp
from jax import lax
from jax.experimental import pallas as pl
from jax.experimental.pallas import tpu as pltpu
from jax.sharding import PartitionSpec as P

HOURS = 24
BANDS = 8
BLD_DEV = 2048
LANES = 128
HALF = LANES // 2
GROUP = 256
AXES = ("plane", "cell", "band")

A_WEIGHTING_DB = [-26.2, -16.1, -8.6, -3.2, 0.0, 1.2, 1.0, -1.1]
GAIN = [1.0, 10.0**0.5, 10.0]
LOG10_E = 0.4342944819032518

QUAD = 4
CHUNKS = ((0, 2), (2, 8))

NT = (((1,), (1,)), ((), ()))
VMEM = pl.BlockSpec(memory_space=pltpu.VMEM)
HBM = pl.BlockSpec(memory_space=pltpu.HBM)


def params(chips):
    return pltpu.CompilerParams(vmem_limit_bytes=min(16 * max(chips // 16, 1), 48) * 1024 * 1024)


def bf(x):
    return x.astype(jnp.bfloat16)


def f32(x):
    return x.astype(jnp.float32)


def three_parts(x):
    hi = f32(bf(x))
    rest = x - hi
    mid = f32(bf(rest))
    return hi, mid, rest - mid


def dot(a, b, dims=(((1,), (0,)), ((), ()))):
    return lax.dot_general(a, b, dims, preferred_element_type=jnp.float32)


def one_hot_columns(index, extent):
    rows = lax.broadcasted_iota(jnp.int32, (extent, index.shape[1]), 0)
    return bf(jnp.where(rows == index, jnp.float32(1.0), jnp.float32(0.0)))


def one_hot_groups(index):
    step = 16
    shape = (step, index.shape[1])
    rows = lax.broadcasted_iota(jnp.int32, shape, 0).astype(jnp.int16)
    wanted = jnp.broadcast_to(index, shape).astype(jnp.int16)
    one, zero = jnp.ones(shape, jnp.bfloat16), jnp.zeros(shape, jnp.bfloat16)
    return jnp.concatenate(
        [jnp.where(wanted == rows + jnp.int16(start), one, zero) for start in range(0, GROUP, step)], axis=0
    )


def merge(low, high):
    lane = lax.broadcasted_iota(jnp.int32, low.shape, 1)
    return jnp.where(lane < HALF, low, high)


def hour_gains(period_row):
    gain = jnp.where(period_row == 0, GAIN[0], jnp.where(period_row == 1, GAIN[1], jnp.where(period_row == 2, GAIN[2], 0.0)))
    shape = (HOURS, HOURS)
    same = lax.broadcasted_iota(jnp.int32, shape, 0) == lax.broadcasted_iota(jnp.int32, shape, 1)
    return jnp.sum(jnp.where(same, jnp.broadcast_to(gain, shape), 0.0), axis=1, keepdims=True)


def band_sums(emission, gains):
    sums = []
    for b in range(BANDS):
        rows = f32(emission[b * HOURS : (b + 1) * HOURS, :])
        factor = 10.0 ** (A_WEIGHTING_DB[b] / 10.0) / HOURS
        sums.append(jnp.sum(rows * (gains * factor), axis=0, keepdims=True))
    total = jnp.concatenate(sums, axis=0)
    high = f32(bf(total))
    return bf(jnp.concatenate([high, total - high], axis=0))


def chunk_rows(i):
    first, last = CHUNKS[i]
    if i == 0:
        return 0, last * HOURS + 2 * BANDS
    return first * HOURS + 2 * BANDS, (last - first) * HOURS


def extend_order(emission, sums):
    cut = CHUNKS[0][1] * HOURS
    return jnp.concatenate([emission[:cut], sums, emission[cut:]], axis=0)


def lists_of(list_ref, step, swapped):
    plane = lax.axis_index("plane") ^ step
    band = lax.axis_index("band")
    order = [q ^ 1 if swapped else q for q in range(QUAD)]
    return jnp.concatenate([list_ref[pl.ds(2 * (plane * QUAD + q) + band, 1), :] for q in order], axis=1)


def own_kernel(period_hbm, emission_hbm, list_hbm, out_ref, period_ref, emission_ref, list_ref, sems):
    pairs = ((list_hbm, list_ref), (period_hbm, period_ref), (emission_hbm, emission_ref))
    copies = [pltpu.make_async_copy(src, dst, sems.at[i]) for i, (src, dst) in enumerate(pairs)]
    for copy in copies:
        copy.start()
    for copy in copies:
        copy.wait()
    emission = emission_ref[...]
    rows = extend_order(emission, band_sums(emission, hour_gains(period_ref[...])))
    for step in range(out_ref.shape[0]):
        found = bf(dot(rows, one_hot_columns(lists_of(list_ref, step, False), rows.shape[1])))
        for pair in range(QUAD // 2):
            out_ref[step, pair] = found[:, pair * LANES : (pair + 1) * LANES]


def other_kernel(period_ref, emission_ref, list_ref, own_ref, *refs):
    planes = own_ref.shape[0]
    a_refs, (b_hbm, b_ref, sems) = refs[:planes], refs[planes:]
    emission = emission_ref[...]
    rows = extend_order(emission, band_sums(emission, hour_gains(period_ref[...])))
    (start_a, count_a), (start_b, count_b) = chunk_rows(0), chunk_rows(1)
    copies = []
    for step in range(planes):
        found = bf(dot(rows, one_hot_columns(lists_of(list_ref, step, True), rows.shape[1])))
        for pair in range(QUAD // 2):
            other = found[:, pair * LANES : (pair + 1) * LANES]
            own = own_ref[step, pair]
            for odd, block in ((0, merge(own, other)), (1, merge(other, own))):
                q = 2 * pair + odd
                a_refs[step][q] = block[start_a : start_a + count_a]
                b_ref[q, step] = block[start_b : start_b + count_b]
        copy = pltpu.make_async_copy(b_ref.at[:, step], b_hbm.at[:, step], sems.at[step])
        copy.start()
        copies.append(copy)
    for copy in copies:
        copy.wait()


def make_sends(hour_period, emission_t, other_t, sends, other_sends, chips):
    width, segs = emission_t.shape
    total = width + 2 * BANDS
    planes = chips // QUAD
    period = hour_period.reshape(1, HOURS)
    operands = [period, emission_t, sends]
    own = pl.pallas_call(
        own_kernel,
        in_specs=[HBM] * 3,
        out_specs=VMEM,
        out_shape=jax.ShapeDtypeStruct((planes, QUAD // 2, total, LANES), jnp.bfloat16),
        scratch_shapes=[pltpu.VMEM(x.shape, x.dtype) for x in operands] + [pltpu.SemaphoreType.DMA((3,))],
        compiler_params=params(chips),
        name="own_rows",
    )(*operands)
    outs = pl.pallas_call(
        other_kernel,
        in_specs=[VMEM] * 4,
        out_specs=[VMEM] * planes + [HBM],
        out_shape=[jax.ShapeDtypeStruct((QUAD, chunk_rows(0)[1], LANES), jnp.bfloat16)] * planes
        + [jax.ShapeDtypeStruct((QUAD, planes, chunk_rows(1)[1], LANES), jnp.bfloat16)],
        scratch_shapes=[
            pltpu.VMEM((QUAD, planes, chunk_rows(1)[1], LANES), jnp.bfloat16),
            pltpu.SemaphoreType.DMA((planes,)),
        ],
        compiler_params=params(chips),
        name="send_rows",
    )(period, other_t, other_sends, own)
    return outs[:planes], outs[planes]


def regroup_kernel(planes, *refs):
    b_ref = refs[1]
    a_refs, a_hbm = refs[2 : planes + 2], refs[planes + 2]
    b_outs, sems = refs[planes + 3 : -1], refs[-1]
    copies = [pltpu.make_async_copy(ref, a_hbm.at[:, j], sems.at[j]) for j, ref in enumerate(a_refs)]
    for copy in copies:
        copy.start()
    for j, out in enumerate(b_outs, 1):
        for q in range(QUAD):
            out[q] = b_ref[q, j]
    for copy in copies:
        copy.wait()


def regroup(after, blocks_a, block_b, chips):
    planes = len(blocks_a)
    outs = pl.pallas_call(
        functools.partial(regroup_kernel, planes),
        in_specs=[VMEM] * (2 + planes),
        out_specs=[HBM] + [VMEM] * (planes - 1),
        out_shape=[jax.ShapeDtypeStruct((QUAD, planes) + blocks_a[0].shape[1:], jnp.bfloat16)]
        + [jax.ShapeDtypeStruct((QUAD,) + block_b.shape[2:], jnp.bfloat16)] * (planes - 1),
        scratch_shapes=[pltpu.SemaphoreType.DMA((planes,))],
        compiler_params=params(chips),
        name="regroup",
    )(after, block_b, *blocks_a)
    return outs[0], outs[1:]


def along_planes(blocks):
    planes = len(blocks) + 1
    return [lax.ppermute(block, "plane", [(p, p ^ j) for p in range(planes)]) for j, block in enumerate(blocks, 1)]


def among_cells(array):
    return lax.all_to_all(array, "cell", split_axis=0, concat_axis=0, tiled=True)


def exchange(blocks_a, block_b, chips, after):
    near_b = among_cells(block_b)
    held_a = [blocks_a[0]] + along_planes(blocks_a[1:])
    grouped_a, grouped_b = regroup(after, held_a, near_b, chips)
    return among_cells(grouped_a), [near_b] + along_planes(grouped_b)


def slot_places(slots):
    half = (lax.axis_index("band") ^ (lax.axis_index("cell") & 1)) * HALF
    return slots ^ (lax.axis_index("plane") * (QUAD * LANES) + half)


def blocks_of_first(ref):
    return [ref.at[q, j] for j in range(ref.shape[1]) for q in range(QUAD)]


def blocks_of_second(refs):
    near, far = refs[0], refs[1:]
    return [near.at[q, 0] for q in range(QUAD)] + [ref.at[q] for ref in far for q in range(QUAD)]


def stack_groups(blocks, start, count, table_ref, first, rows):
    per_group = GROUP // LANES
    for c, block in enumerate(blocks):
        g, j = divmod(c, per_group)
        table_ref[pl.ds(g * rows + first, count), j * LANES : (j + 1) * LANES] = block[start : start + count, :]


def index_kernel(after_ref, slots_ref, dwell_ref, addr_ref, building_ref, places_out, dwell_out, addr_out, building_out):
    places_out[...] = slot_places(slots_ref[...])
    dwell_out[...] = f32(dwell_ref[...])
    for ref, out in ((addr_ref, addr_out), (building_ref, building_out)):
        out[...] = jnp.concatenate([ref[c : c + 1, :] for c in range(ref.shape[0])], axis=1)


def make_index(after, tile_slots, dwellings, addr_t, building_t, chips):
    dwell = dwellings.reshape(-1, LANES)
    row = jax.ShapeDtypeStruct((1, addr_t.size), jnp.int32)
    return pl.pallas_call(
        index_kernel,
        in_specs=[HBM] + [VMEM] * 4,
        out_specs=[VMEM] * 4,
        out_shape=[
            jax.ShapeDtypeStruct(tile_slots.shape, jnp.int32),
            jax.ShapeDtypeStruct(dwell.shape, jnp.float32),
            row,
            row,
        ],
        compiler_params=params(chips),
        name="index_rows",
    )(after, tile_slots, dwell, addr_t, building_t)


def gather_columns(table, rows, places):
    found = dot(table, one_hot_groups(places & (GROUP - 1)))
    group = places >> (GROUP.bit_length() - 1)
    out = jnp.zeros((rows, places.shape[1]), jnp.float32)
    for g in range(table.shape[0] // rows):
        out = jnp.where(group == g, found[g * rows : (g + 1) * rows], out)
    return out


def level_kernel(devices, recv_ref, places_ref, absorption_ref, geometry_ref, dwell_ref, addr_ref, *refs):
    level_ref, pay_hbm, table, pay_ref, sem = refs
    blocks = blocks_of_first(recv_ref)
    tiles, recv_tile, paths = geometry_ref.shape
    rows = 2 * BANDS
    stack_groups(blocks, blocks[0].shape[0] - rows, rows, table, 0, rows)
    places = places_ref[...]
    per_tile = recv_tile // LANES
    zeros = jnp.zeros((5, paths), jnp.float32)
    for t in range(tiles):
        sums = gather_columns(table[...], rows, places[t : t + 1, :])
        path = jnp.sum(f32(absorption_ref[t]) * (sums[:BANDS] + sums[BANDS:]), axis=0, keepdims=True)
        lhs = bf(jnp.concatenate([*three_parts(path), zeros], axis=0))
        energy = jnp.sum(dot(lhs, geometry_ref[t], NT), axis=0, keepdims=True)
        level = jnp.log(energy) * LOG10_E
        for j in range(per_tile):
            level_ref[t * per_tile + j : t * per_tile + j + 1, :] = level[:, j * LANES : (j + 1) * LANES]

    addr = addr_ref[...]
    cap = addr.shape[1] // devices
    level_rows = level_ref.shape[0]
    parts = [*three_parts(level_ref[...]), dwell_ref[...]]
    found = dot(bf(jnp.concatenate(parts, axis=0)), one_hot_columns(addr & (LANES - 1), LANES))
    row = lax.broadcasted_iota(jnp.int32, (level_rows, addr.shape[1]), 0)
    hit = row == (addr >> (LANES.bit_length() - 1))

    def pick(i):
        part = found[i * level_rows : (i + 1) * level_rows]
        return jnp.sum(jnp.where(hit, part, 0.0), axis=0, keepdims=True)

    dwelt = pick(3)
    weighted = dwelt * ((pick(0) + pick(1)) + pick(2))
    lines = [value[:, c * devices : (c + 1) * devices] for value in (weighted, dwelt) for c in range(cap)]
    square = jnp.concatenate(lines + [jnp.zeros((LANES - 2 * cap, devices), jnp.float32)], axis=0)
    if devices < LANES:
        square = jnp.concatenate([square, jnp.zeros((LANES, LANES - devices), jnp.float32)], axis=1)
    turned = square.T
    for d in range(devices):
        pay_ref[d] = turned[d : d + 1, :]
    copy = pltpu.make_async_copy(pay_ref, pay_hbm, sem)
    copy.start()
    copy.wait()


def make_levels(recv, chips, places, absorption, geometry, dwell, addr):
    tiles, recv_tile, paths = geometry.shape
    devices = 2 * chips
    operands = [recv, places, absorption, geometry, dwell, addr]
    return pl.pallas_call(
        functools.partial(level_kernel, devices),
        in_specs=[VMEM] * len(operands),
        out_specs=[VMEM, HBM],
        out_shape=[
            jax.ShapeDtypeStruct(dwell.shape, jnp.float32),
            jax.ShapeDtypeStruct((devices, 1, LANES), jnp.float32),
        ],
        scratch_shapes=[
            pltpu.VMEM((chips * LANES // GROUP * 2 * BANDS, GROUP), jnp.bfloat16),
            pltpu.VMEM((devices, 1, LANES), jnp.float32),
            pltpu.SemaphoreType.DMA,
        ],
        compiler_params=params(chips),
        name="levels",
    )(*operands)


def exposure_kernel(planes, *refs):
    places_ref, absorption_ref, geometry_ref, out_hbm, done_ref, table, out_ref, sems = refs[1 + planes :]
    done_ref[...] = jnp.zeros_like(done_ref)
    tiles, recv_tile, paths = geometry_ref.shape
    rows = out_ref.shape[0]
    for (first, last), blocks in zip(CHUNKS, (blocks_of_first(refs[0]), blocks_of_second(refs[1 : 1 + planes]))):
        stack_groups(blocks, 0, (last - first) * HOURS, table, first * HOURS, rows)
    places = places_ref[...]
    copies = []
    for t in range(tiles):
        gathered = gather_columns(table[...], rows, places[t : t + 1, :])
        absorption = f32(absorption_ref[t])
        mixed = jnp.concatenate(
            [absorption[b : b + 1] * gathered[b * HOURS : (b + 1) * HOURS] for b in range(BANDS)], axis=0
        )
        columns = slice(t * recv_tile, (t + 1) * recv_tile)
        out_ref[:, columns] = dot(bf(mixed), geometry_ref[t], NT)
        copy = pltpu.make_async_copy(out_ref.at[:, columns], out_hbm.at[:, columns], sems.at[t])
        copy.start()
        copies.append(copy)
    for copy in copies:
        copy.wait()


def make_exposure(moved, chips, places, absorption, geometry):
    tiles, recv_tile, paths = geometry.shape
    shape = (BANDS * HOURS, tiles * recv_tile)
    operands = [moved[0], *moved[1], places, absorption, geometry]
    return pl.pallas_call(
        functools.partial(exposure_kernel, chips // QUAD),
        in_specs=[VMEM] * len(operands),
        out_specs=[HBM, VMEM],
        out_shape=[jax.ShapeDtypeStruct(shape, jnp.float32), jax.ShapeDtypeStruct((8, LANES), jnp.float32)],
        scratch_shapes=[
            pltpu.VMEM((chips * LANES // GROUP * shape[0], GROUP), jnp.bfloat16),
            pltpu.VMEM(shape, jnp.float32),
            pltpu.SemaphoreType.DMA((tiles,)),
        ],
        compiler_params=params(chips),
        name="exposure",
    )(*operands)


def building_kernel(after_ref, arrived_ref, building_ref, out_ref):
    devices = arrived_ref.shape[0]
    building = building_ref[...]
    cap = building.shape[1] // devices
    square = jnp.concatenate([arrived_ref[s] for s in range(devices)], axis=0)
    if devices < LANES:
        square = jnp.concatenate([square, jnp.zeros((LANES - devices, LANES), jnp.float32)], axis=0)
    turned = square.T

    def line(ref, first):
        return jnp.concatenate([ref[first + c : first + c + 1, :devices] for c in range(cap)], axis=1)

    weighted, dwelt = line(turned, 0), line(turned, cap)
    rows = out_ref.shape[0]
    row = lax.broadcasted_iota(jnp.int32, (rows, building.shape[1]), 0)
    hit = row == (building >> (LANES.bit_length() - 1))
    parts = [jnp.where(hit, value, 0.0) for value in three_parts(weighted) + (dwelt,)]
    table = one_hot_columns(building & (LANES - 1), LANES)
    sums = dot(bf(jnp.concatenate(parts, axis=0)), table, NT)
    numer = (sums[:rows] + sums[rows : 2 * rows]) + sums[2 * rows : 3 * rows]
    out_ref[...] = numer / jnp.maximum(sums[3 * rows :], 1.0)


def make_buildings(after, arrived, building, chips):
    return pl.pallas_call(
        building_kernel,
        in_specs=[VMEM] * 3,
        out_specs=VMEM,
        out_shape=jax.ShapeDtypeStruct((BLD_DEV // LANES, LANES), jnp.float32),
        compiler_params=params(chips),
        name="buildings",
    )(after, arrived, building)


def local(
    emission,
    path_sends,
    tile_slots,
    geometry,
    absorption,
    hour_period,
    dwellings,
    addr_sends,
    addr_building,
    chips,
):
    swap = [(0, 1), (1, 0)]
    emission_t = emission.T
    sends = path_sends[0]
    other_t = lax.ppermute(emission_t, "band", swap)
    other_sends = lax.ppermute(sends, "band", swap)
    blocks_a, block_b = make_sends(hour_period, emission_t, other_t, sends, other_sends, chips)
    places, dwell, addr, building = make_index(
        blocks_a[0], tile_slots, dwellings, addr_sends[0].T, addr_building[0].T, chips
    )
    moved = exchange(blocks_a, block_b, chips, places)
    levels, pay = make_levels(moved[0], chips, places, absorption, geometry, dwell, addr)
    arrived = lax.all_to_all(pay, AXES, split_axis=0, concat_axis=0, tiled=True)
    exposure_t, done = make_exposure(moved, chips, places, absorption, geometry)
    buildings = make_buildings(done, arrived, building, chips)
    return (levels.reshape(-1), buildings.reshape(-1), exposure_t.T)


def solution(mesh):
    chips = mesh.shape["region"]
    cells = jax.sharding.Mesh(mesh.devices.reshape(chips // QUAD, QUAD, mesh.shape["band"]), AXES)
    in_specs = (
        P(AXES, None),
        P(AXES, None, None),
        P(AXES, None),
        P(AXES, None, None),
        P(AXES, None, None),
        P(),
        P(AXES),
        P(AXES, None, None),
        P(AXES, None, None),
    )
    out_specs = (P(AXES), P(AXES), P(AXES, None))
    body = functools.partial(local, chips=chips)
    return jax.shard_map(body, mesh=cells, in_specs=in_specs, out_specs=out_specs, check_vma=False)
```

```python
import functools

import jax
import jax.numpy as jnp
from jax import lax
from jax.experimental import pallas as pl
from jax.experimental.pallas import tpu as pltpu
from jax.sharding import PartitionSpec as P

HOURS = 24
BANDS = 8
BLD_DEV = 2048
LANES = 128
HALF = LANES // 2
GROUP = 256
AXES = ("plane", "cell", "band")

A_WEIGHTING_DB = [-26.2, -16.1, -8.6, -3.2, 0.0, 1.2, 1.0, -1.1]
GAIN = [1.0, 10.0**0.5, 10.0]
LOG10_E = 0.4342944819032518

QUAD = 4
CHUNKS = ((0, 2), (2, 8))

NT = (((1,), (1,)), ((), ()))
VMEM = pl.BlockSpec(memory_space=pltpu.VMEM)
HBM = pl.BlockSpec(memory_space=pltpu.HBM)


def params(chips):
    return pltpu.CompilerParams(vmem_limit_bytes=min(16 * max(chips // 16, 1), 48) * 1024 * 1024)


def bf(x):
    return x.astype(jnp.bfloat16)


def f32(x):
    return x.astype(jnp.float32)


def three_parts(x):
    hi = f32(bf(x))
    rest = x - hi
    mid = f32(bf(rest))
    return hi, mid, rest - mid


def dot(a, b, dims=(((1,), (0,)), ((), ()))):
    return lax.dot_general(a, b, dims, preferred_element_type=jnp.float32)


def one_hot_columns(index, extent):
    rows = lax.broadcasted_iota(jnp.int32, (extent, index.shape[1]), 0)
    return bf(jnp.where(rows == index, jnp.float32(1.0), jnp.float32(0.0)))


def one_hot_groups(index):
    step = 16
    shape = (step, index.shape[1])
    rows = lax.broadcasted_iota(jnp.int32, shape, 0).astype(jnp.int16)
    wanted = jnp.broadcast_to(index, shape).astype(jnp.int16)
    one, zero = jnp.ones(shape, jnp.bfloat16), jnp.zeros(shape, jnp.bfloat16)
    return jnp.concatenate(
        [jnp.where(wanted == rows + jnp.int16(start), one, zero) for start in range(0, GROUP, step)], axis=0
    )


def merge(low, high):
    lane = lax.broadcasted_iota(jnp.int32, low.shape, 1)
    return jnp.where(lane < HALF, low, high)


def hour_gains(period_row):
    gain = jnp.where(period_row == 0, GAIN[0], jnp.where(period_row == 1, GAIN[1], jnp.where(period_row == 2, GAIN[2], 0.0)))
    shape = (HOURS, HOURS)
    same = lax.broadcasted_iota(jnp.int32, shape, 0) == lax.broadcasted_iota(jnp.int32, shape, 1)
    return jnp.sum(jnp.where(same, jnp.broadcast_to(gain, shape), 0.0), axis=1, keepdims=True)


def band_sums(emission, gains):
    sums = []
    for b in range(BANDS):
        rows = f32(emission[b * HOURS : (b + 1) * HOURS, :])
        factor = 10.0 ** (A_WEIGHTING_DB[b] / 10.0) / HOURS
        sums.append(jnp.sum(rows * (gains * factor), axis=0, keepdims=True))
    total = jnp.concatenate(sums, axis=0)
    high = f32(bf(total))
    return bf(jnp.concatenate([high, total - high], axis=0))


def chunk_rows(i):
    first, last = CHUNKS[i]
    if i == 0:
        return 0, last * HOURS + 2 * BANDS
    return first * HOURS + 2 * BANDS, (last - first) * HOURS


def extend_order(emission, sums):
    cut = CHUNKS[0][1] * HOURS
    return jnp.concatenate([emission[:cut], sums, emission[cut:]], axis=0)


def turned_step(step):
    low, high = step & 1, (step >> 1) & 1
    return (step & ~3) | (((low ^ high) << 1) | high)


def turned_back(step):
    low, high = step & 1, (step >> 1) & 1
    return (step & ~3) | ((low << 1) | (low ^ high))


def lists_of(list_ref, step, swapped):
    plane = lax.axis_index("plane") ^ jnp.where(lax.axis_index("band") == 0, step, turned_step(step))
    band = lax.axis_index("band")
    order = [q ^ 1 if swapped else q for q in range(QUAD)]
    return jnp.concatenate([list_ref[pl.ds(2 * (plane * QUAD + q) + band, 1), :] for q in order], axis=1)


def own_kernel(period_hbm, emission_hbm, list_hbm, out_ref, period_ref, emission_ref, list_ref, sems):
    pairs = ((list_hbm, list_ref), (period_hbm, period_ref), (emission_hbm, emission_ref))
    copies = [pltpu.make_async_copy(src, dst, sems.at[i]) for i, (src, dst) in enumerate(pairs)]
    for copy in copies:
        copy.start()
    for copy in copies:
        copy.wait()
    emission = emission_ref[...]
    rows = extend_order(emission, band_sums(emission, hour_gains(period_ref[...])))
    for step in range(out_ref.shape[0]):
        found = bf(dot(rows, one_hot_columns(lists_of(list_ref, step, False), rows.shape[1])))
        for pair in range(QUAD // 2):
            out_ref[step, pair] = found[:, pair * LANES : (pair + 1) * LANES]


def other_kernel(period_ref, emission_ref, list_ref, own_ref, *refs):
    planes = own_ref.shape[0]
    a_refs, (b_hbm, b_ref, sems) = refs[:planes], refs[planes:]
    emission = emission_ref[...]
    rows = extend_order(emission, band_sums(emission, hour_gains(period_ref[...])))
    (start_a, count_a), (start_b, count_b) = chunk_rows(0), chunk_rows(1)
    copies = []
    for step in range(planes):
        found = bf(dot(rows, one_hot_columns(lists_of(list_ref, step, True), rows.shape[1])))
        for pair in range(QUAD // 2):
            other = found[:, pair * LANES : (pair + 1) * LANES]
            own = own_ref[step, pair]
            for odd, block in ((0, merge(own, other)), (1, merge(other, own))):
                q = 2 * pair + odd
                a_refs[step][q] = block[start_a : start_a + count_a]
                b_ref[q, step] = block[start_b : start_b + count_b]
        copy = pltpu.make_async_copy(b_ref.at[:, step], b_hbm.at[:, step], sems.at[step])
        copy.start()
        copies.append(copy)
    for copy in copies:
        copy.wait()


def make_sends(hour_period, emission_t, other_t, sends, other_sends, chips):
    width, segs = emission_t.shape
    total = width + 2 * BANDS
    planes = chips // QUAD
    period = hour_period.reshape(1, HOURS)
    operands = [period, emission_t, sends]
    own = pl.pallas_call(
        own_kernel,
        in_specs=[HBM] * 3,
        out_specs=VMEM,
        out_shape=jax.ShapeDtypeStruct((planes, QUAD // 2, total, LANES), jnp.bfloat16),
        scratch_shapes=[pltpu.VMEM(x.shape, x.dtype) for x in operands] + [pltpu.SemaphoreType.DMA((3,))],
        compiler_params=params(chips),
        name="own_rows",
    )(*operands)
    outs = pl.pallas_call(
        other_kernel,
        in_specs=[VMEM] * 4,
        out_specs=[VMEM] * planes + [HBM],
        out_shape=[jax.ShapeDtypeStruct((QUAD, chunk_rows(0)[1], LANES), jnp.bfloat16)] * planes
        + [jax.ShapeDtypeStruct((QUAD, planes, chunk_rows(1)[1], LANES), jnp.bfloat16)],
        scratch_shapes=[
            pltpu.VMEM((QUAD, planes, chunk_rows(1)[1], LANES), jnp.bfloat16),
            pltpu.SemaphoreType.DMA((planes,)),
        ],
        compiler_params=params(chips),
        name="send_rows",
    )(period, other_t, other_sends, own)
    return outs[:planes], outs[planes]


def regroup_kernel(planes, *refs):
    b_ref = refs[1]
    a_refs, a_hbm = refs[2 : planes + 2], refs[planes + 2]
    b_outs, sems = refs[planes + 3 : -1], refs[-1]
    copies = [pltpu.make_async_copy(ref, a_hbm.at[:, j], sems.at[j]) for j, ref in enumerate(a_refs)]
    for copy in copies:
        copy.start()
    for j, out in enumerate(b_outs, 1):
        for q in range(QUAD):
            out[q] = b_ref[q, j]
    for copy in copies:
        copy.wait()


def regroup(after, blocks_a, block_b, chips):
    planes = len(blocks_a)
    outs = pl.pallas_call(
        functools.partial(regroup_kernel, planes),
        in_specs=[VMEM] * (2 + planes),
        out_specs=[HBM] + [VMEM] * (planes - 1),
        out_shape=[jax.ShapeDtypeStruct((QUAD, planes) + blocks_a[0].shape[1:], jnp.bfloat16)]
        + [jax.ShapeDtypeStruct((QUAD,) + block_b.shape[2:], jnp.bfloat16)] * (planes - 1),
        scratch_shapes=[pltpu.SemaphoreType.DMA((planes,))],
        compiler_params=params(chips),
        name="regroup",
    )(after, block_b, *blocks_a)
    return outs[0], outs[1:]


def along_planes(blocks):
    planes = len(blocks) + 1

    def pairs(step):
        return [(2 * p + core, 2 * (p ^ own) + core) for core, own in enumerate((step, turned_step(step))) for p in range(planes)]

    return [lax.ppermute(block, ("plane", "band"), pairs(step)) for step, block in enumerate(blocks, 1)]


def among_cells(array):
    return lax.all_to_all(array, "cell", split_axis=0, concat_axis=0, tiled=True)


def exchange(blocks_a, block_b, chips, after):
    near_b = among_cells(block_b)
    held_a = [blocks_a[0]] + along_planes(blocks_a[1:])
    grouped_a, grouped_b = regroup(after, held_a, near_b, chips)
    return among_cells(grouped_a), [near_b] + along_planes(grouped_b)


def slot_places(slots):
    half = (lax.axis_index("band") ^ (lax.axis_index("cell") & 1)) * HALF
    shift = (QUAD * LANES).bit_length() - 1
    place = slots ^ ((lax.axis_index("plane") << shift) + half)
    turned = (turned_back(place >> shift) << shift) | (place & (QUAD * LANES - 1))
    return jnp.where(lax.axis_index("band") == 0, place, turned)


def blocks_of_first(ref):
    return [ref.at[q, j] for j in range(ref.shape[1]) for q in range(QUAD)]


def blocks_of_second(refs):
    near, far = refs[0], refs[1:]
    return [near.at[q, 0] for q in range(QUAD)] + [ref.at[q] for ref in far for q in range(QUAD)]


def stack_groups(blocks, start, count, table_ref, first, rows):
    per_group = GROUP // LANES
    for c, block in enumerate(blocks):
        g, j = divmod(c, per_group)
        table_ref[pl.ds(g * rows + first, count), j * LANES : (j + 1) * LANES] = block[start : start + count, :]


def index_kernel(after_ref, slots_ref, dwell_ref, addr_ref, building_ref, places_out, dwell_out, addr_out, building_out):
    places_out[...] = slot_places(slots_ref[...])
    dwell_out[...] = f32(dwell_ref[...])
    for ref, out in ((addr_ref, addr_out), (building_ref, building_out)):
        out[...] = jnp.concatenate([ref[c : c + 1, :] for c in range(ref.shape[0])], axis=1)


def make_index(after, tile_slots, dwellings, addr_t, building_t, chips):
    dwell = dwellings.reshape(-1, LANES)
    row = jax.ShapeDtypeStruct((1, addr_t.size), jnp.int32)
    return pl.pallas_call(
        index_kernel,
        in_specs=[HBM] + [VMEM] * 4,
        out_specs=[VMEM] * 4,
        out_shape=[
            jax.ShapeDtypeStruct(tile_slots.shape, jnp.int32),
            jax.ShapeDtypeStruct(dwell.shape, jnp.float32),
            row,
            row,
        ],
        compiler_params=params(chips),
        name="index_rows",
    )(after, tile_slots, dwell, addr_t, building_t)


def gather_columns(table, rows, places):
    found = dot(table, one_hot_groups(places & (GROUP - 1)))
    group = places >> (GROUP.bit_length() - 1)
    out = jnp.zeros((rows, places.shape[1]), jnp.float32)
    for g in range(table.shape[0] // rows):
        out = jnp.where(group == g, found[g * rows : (g + 1) * rows], out)
    return out


def level_kernel(devices, recv_ref, places_ref, absorption_ref, geometry_ref, dwell_ref, addr_ref, *refs):
    level_ref, pay_ref, table = refs
    blocks = blocks_of_first(recv_ref)
    tiles, recv_tile, paths = geometry_ref.shape
    rows = 2 * BANDS
    stack_groups(blocks, blocks[0].shape[0] - rows, rows, table, 0, rows)
    places = places_ref[...]
    per_tile = recv_tile // LANES
    zeros = jnp.zeros((5, paths), jnp.float32)
    for t in range(tiles):
        sums = gather_columns(table[...], rows, places[t : t + 1, :])
        path = jnp.sum(f32(absorption_ref[t]) * (sums[:BANDS] + sums[BANDS:]), axis=0, keepdims=True)
        lhs = bf(jnp.concatenate([*three_parts(path), zeros], axis=0))
        energy = jnp.sum(dot(lhs, geometry_ref[t], NT), axis=0, keepdims=True)
        level = jnp.log(energy) * LOG10_E
        for j in range(per_tile):
            level_ref[t * per_tile + j : t * per_tile + j + 1, :] = level[:, j * LANES : (j + 1) * LANES]

    addr = addr_ref[...]
    cap = addr.shape[1] // devices
    level_rows = level_ref.shape[0]
    parts = [*three_parts(level_ref[...]), dwell_ref[...]]
    found = dot(bf(jnp.concatenate(parts, axis=0)), one_hot_columns(addr & (LANES - 1), LANES))
    row = lax.broadcasted_iota(jnp.int32, (level_rows, addr.shape[1]), 0)
    hit = row == (addr >> (LANES.bit_length() - 1))

    def pick(i):
        part = found[i * level_rows : (i + 1) * level_rows]
        return jnp.sum(jnp.where(hit, part, 0.0), axis=0, keepdims=True)

    dwelt = pick(3)
    weighted = dwelt * ((pick(0) + pick(1)) + pick(2))
    lines = [value[:, c * devices : (c + 1) * devices] for value in (weighted, dwelt) for c in range(cap)]
    square = jnp.concatenate(lines + [jnp.zeros((LANES - 2 * cap, devices), jnp.float32)], axis=0)
    if devices < LANES:
        square = jnp.concatenate([square, jnp.zeros((LANES, LANES - devices), jnp.float32)], axis=1)
    turned = square.T
    for d in range(devices):
        pay_ref[d] = turned[d : d + 1, :]


def make_levels(recv, chips, places, absorption, geometry, dwell, addr):
    tiles, recv_tile, paths = geometry.shape
    devices = 2 * chips
    operands = [recv, places, absorption, geometry, dwell, addr]
    return pl.pallas_call(
        functools.partial(level_kernel, devices),
        in_specs=[VMEM] * len(operands),
        out_specs=[VMEM] * 2,
        out_shape=[
            jax.ShapeDtypeStruct(dwell.shape, jnp.float32),
            jax.ShapeDtypeStruct((devices, 1, LANES), jnp.float32),
        ],
        scratch_shapes=[pltpu.VMEM((chips * LANES // GROUP * 2 * BANDS, GROUP), jnp.bfloat16)],
        compiler_params=params(chips),
        name="levels",
    )(*operands)


def exposure_kernel(planes, *refs):
    places_ref, absorption_ref, geometry_ref, out_hbm, done_ref, table, out_ref, sems = refs[1 + planes :]
    done_ref[...] = jnp.zeros_like(done_ref)
    tiles, recv_tile, paths = geometry_ref.shape
    rows = out_ref.shape[0]
    for (first, last), blocks in zip(CHUNKS, (blocks_of_first(refs[0]), blocks_of_second(refs[1 : 1 + planes]))):
        stack_groups(blocks, 0, (last - first) * HOURS, table, first * HOURS, rows)
    places = places_ref[...]
    copies = []
    for t in range(tiles):
        gathered = gather_columns(table[...], rows, places[t : t + 1, :])
        absorption = f32(absorption_ref[t])
        mixed = jnp.concatenate(
            [absorption[b : b + 1] * gathered[b * HOURS : (b + 1) * HOURS] for b in range(BANDS)], axis=0
        )
        columns = slice(t * recv_tile, (t + 1) * recv_tile)
        out_ref[:, columns] = dot(bf(mixed), geometry_ref[t], NT)
        copy = pltpu.make_async_copy(out_ref.at[:, columns], out_hbm.at[:, columns], sems.at[t])
        copy.start()
        copies.append(copy)
    for copy in copies:
        copy.wait()


def make_exposure(moved, chips, places, absorption, geometry):
    tiles, recv_tile, paths = geometry.shape
    shape = (BANDS * HOURS, tiles * recv_tile)
    operands = [moved[0], *moved[1], places, absorption, geometry]
    return pl.pallas_call(
        functools.partial(exposure_kernel, chips // QUAD),
        in_specs=[VMEM] * len(operands),
        out_specs=[HBM, VMEM],
        out_shape=[jax.ShapeDtypeStruct(shape, jnp.float32), jax.ShapeDtypeStruct((8, LANES), jnp.float32)],
        scratch_shapes=[
            pltpu.VMEM((chips * LANES // GROUP * shape[0], GROUP), jnp.bfloat16),
            pltpu.VMEM(shape, jnp.float32),
            pltpu.SemaphoreType.DMA((tiles,)),
        ],
        compiler_params=params(chips),
        name="exposure",
    )(*operands)


def building_kernel(after_ref, arrived_ref, building_ref, out_ref):
    devices = arrived_ref.shape[0]
    building = building_ref[...]
    cap = building.shape[1] // devices
    square = jnp.concatenate([arrived_ref[s] for s in range(devices)], axis=0)
    if devices < LANES:
        square = jnp.concatenate([square, jnp.zeros((LANES - devices, LANES), jnp.float32)], axis=0)
    turned = square.T

    def line(ref, first):
        return jnp.concatenate([ref[first + c : first + c + 1, :devices] for c in range(cap)], axis=1)

    weighted, dwelt = line(turned, 0), line(turned, cap)
    rows = out_ref.shape[0]
    row = lax.broadcasted_iota(jnp.int32, (rows, building.shape[1]), 0)
    hit = row == (building >> (LANES.bit_length() - 1))
    parts = [jnp.where(hit, value, 0.0) for value in three_parts(weighted) + (dwelt,)]
    table = one_hot_columns(building & (LANES - 1), LANES)
    sums = dot(bf(jnp.concatenate(parts, axis=0)), table, NT)
    numer = (sums[:rows] + sums[rows : 2 * rows]) + sums[2 * rows : 3 * rows]
    out_ref[...] = numer / jnp.maximum(sums[3 * rows :], 1.0)


def make_buildings(after, arrived, building, chips):
    return pl.pallas_call(
        building_kernel,
        in_specs=[VMEM] * 3,
        out_specs=VMEM,
        out_shape=jax.ShapeDtypeStruct((BLD_DEV // LANES, LANES), jnp.float32),
        compiler_params=params(chips),
        name="buildings",
    )(after, arrived, building)


def local(
    emission,
    path_sends,
    tile_slots,
    geometry,
    absorption,
    hour_period,
    dwellings,
    addr_sends,
    addr_building,
    chips,
):
    swap = [(0, 1), (1, 0)]
    emission_t = emission.T
    sends = path_sends[0]
    other_t = lax.ppermute(emission_t, "band", swap)
    other_sends = lax.ppermute(sends, "band", swap)
    blocks_a, block_b = make_sends(hour_period, emission_t, other_t, sends, other_sends, chips)
    places, dwell, addr, building = make_index(
        blocks_a[0], tile_slots, dwellings, addr_sends[0].T, addr_building[0].T, chips
    )
    moved = exchange(blocks_a, block_b, chips, places)
    levels, pay = make_levels(moved[0], chips, places, absorption, geometry, dwell, addr)
    arrived = lax.all_to_all(pay, AXES, split_axis=0, concat_axis=0, tiled=True)
    exposure_t, done = make_exposure(moved, chips, places, absorption, geometry)
    buildings = make_buildings(done, arrived, building, chips)
    return (levels.reshape(-1), buildings.reshape(-1), exposure_t.T)


def solution(mesh):
    chips = mesh.shape["region"]
    cells = jax.sharding.Mesh(mesh.devices.reshape(chips // QUAD, QUAD, mesh.shape["band"]), AXES)
    in_specs = (
        P(AXES, None),
        P(AXES, None, None),
        P(AXES, None),
        P(AXES, None, None),
        P(AXES, None, None),
        P(),
        P(AXES),
        P(AXES, None, None),
        P(AXES, None, None),
    )
    out_specs = (P(AXES), P(AXES), P(AXES, None))
    body = functools.partial(local, chips=chips)
    return jax.shard_map(body, mesh=cells, in_specs=in_specs, out_specs=out_specs, check_vma=False)
```

```python
import functools

import jax
import jax.numpy as jnp
from jax import lax
from jax.experimental import pallas as pl
from jax.experimental.pallas import tpu as pltpu
from jax.sharding import PartitionSpec as P

HOURS = 24
BANDS = 8
BLD_DEV = 2048
LANES = 128
HALF = LANES // 2
GROUP = 256
AXES = ("plane", "cell", "band")

A_WEIGHTING_DB = [-26.2, -16.1, -8.6, -3.2, 0.0, 1.2, 1.0, -1.1]
GAIN = [1.0, 10.0**0.5, 10.0]
LOG10_E = 0.4342944819032518

QUAD = 4
CHUNKS = ((0, 2), (2, 8))

NT = (((1,), (1,)), ((), ()))
VMEM = pl.BlockSpec(memory_space=pltpu.VMEM)
HBM = pl.BlockSpec(memory_space=pltpu.HBM)


def params(chips):
    return pltpu.CompilerParams(vmem_limit_bytes=min(16 * max(chips // 16, 1), 48) * 1024 * 1024)


def bf(x):
    return x.astype(jnp.bfloat16)


def f32(x):
    return x.astype(jnp.float32)


def three_parts(x):
    hi = f32(bf(x))
    rest = x - hi
    mid = f32(bf(rest))
    return hi, mid, rest - mid


def dot(a, b, dims=(((1,), (0,)), ((), ()))):
    return lax.dot_general(a, b, dims, preferred_element_type=jnp.float32)


def one_hot_columns(index, extent):
    rows = lax.broadcasted_iota(jnp.int32, (extent, index.shape[1]), 0)
    return bf(jnp.where(rows == index, jnp.float32(1.0), jnp.float32(0.0)))


def one_hot_groups(index):
    step = 16
    shape = (step, index.shape[1])
    rows = lax.broadcasted_iota(jnp.int32, shape, 0).astype(jnp.int16)
    wanted = jnp.broadcast_to(index, shape).astype(jnp.int16)
    one, zero = jnp.ones(shape, jnp.bfloat16), jnp.zeros(shape, jnp.bfloat16)
    return jnp.concatenate(
        [jnp.where(wanted == rows + jnp.int16(start), one, zero) for start in range(0, GROUP, step)], axis=0
    )


def merge(low, high):
    lane = lax.broadcasted_iota(jnp.int32, low.shape, 1)
    return jnp.where(lane < HALF, low, high)


def hour_gains(period_row):
    gain = jnp.where(period_row == 0, GAIN[0], jnp.where(period_row == 1, GAIN[1], jnp.where(period_row == 2, GAIN[2], 0.0)))
    shape = (HOURS, HOURS)
    same = lax.broadcasted_iota(jnp.int32, shape, 0) == lax.broadcasted_iota(jnp.int32, shape, 1)
    return jnp.sum(jnp.where(same, jnp.broadcast_to(gain, shape), 0.0), axis=1, keepdims=True)


def band_sums(emission, gains):
    sums = []
    for b in range(BANDS):
        rows = f32(emission[b * HOURS : (b + 1) * HOURS, :])
        factor = 10.0 ** (A_WEIGHTING_DB[b] / 10.0) / HOURS
        sums.append(jnp.sum(rows * (gains * factor), axis=0, keepdims=True))
    total = jnp.concatenate(sums, axis=0)
    high = f32(bf(total))
    return bf(jnp.concatenate([high, total - high], axis=0))


def chunk_rows(i):
    first, last = CHUNKS[i]
    if i == 0:
        return 0, last * HOURS + 2 * BANDS
    return first * HOURS + 2 * BANDS, (last - first) * HOURS


def turned_step(step):
    low, high = step & 1, (step >> 1) & 1
    return (step & ~3) | (((low ^ high) << 1) | high)


def turned_back(step):
    low, high = step & 1, (step >> 1) & 1
    return (step & ~3) | ((low << 1) | (low ^ high))


def lists_of(list_ref, step, swapped):
    plane = lax.axis_index("plane") ^ jnp.where(lax.axis_index("band") == 0, step, turned_step(step))
    band = lax.axis_index("band")
    order = [q ^ 1 if swapped else q for q in range(QUAD)]
    return jnp.concatenate([list_ref[pl.ds(2 * (plane * QUAD + q) + band, 1), :] for q in order], axis=1)


def own_kernel(emission_hbm, list_hbm, out_ref, emission_ref, list_ref, sems):
    pairs = ((list_hbm, list_ref), (emission_hbm, emission_ref))
    copies = [pltpu.make_async_copy(src, dst, sems.at[i]) for i, (src, dst) in enumerate(pairs)]
    for copy in copies:
        copy.start()
    for copy in copies:
        copy.wait()
    rows = emission_ref[...]
    for step in range(out_ref.shape[0]):
        found = bf(dot(rows, one_hot_columns(lists_of(list_ref, step, False), rows.shape[1])))
        for pair in range(QUAD // 2):
            out_ref[step, pair] = found[:, pair * LANES : (pair + 1) * LANES]


def other_kernel(period_ref, emission_ref, list_ref, own_ref, *refs):
    planes = own_ref.shape[0]
    a_refs, (b_hbm, b_ref, sems) = refs[:planes], refs[planes:]
    rows = emission_ref[...]
    gains = hour_gains(period_ref[...])
    cut = CHUNKS[0][1] * HOURS
    copies = []
    for step in range(planes):
        found = bf(dot(rows, one_hot_columns(lists_of(list_ref, step, True), rows.shape[1])))
        for pair in range(QUAD // 2):
            other = found[:, pair * LANES : (pair + 1) * LANES]
            own = own_ref[step, pair]
            for odd, block in ((0, merge(own, other)), (1, merge(other, own))):
                q = 2 * pair + odd
                a_refs[step][q] = jnp.concatenate([block[:cut], band_sums(block, gains)], axis=0)
                b_ref[q, step] = block[cut:]
        copy = pltpu.make_async_copy(b_ref.at[:, step], b_hbm.at[:, step], sems.at[step])
        copy.start()
        copies.append(copy)
    for copy in copies:
        copy.wait()


def make_sends(period, emission_t, other_t, sends, other_sends, chips):
    width, segs = emission_t.shape
    planes = chips // QUAD
    operands = [emission_t, sends]
    own = pl.pallas_call(
        own_kernel,
        in_specs=[HBM] * 2,
        out_specs=VMEM,
        out_shape=jax.ShapeDtypeStruct((planes, QUAD // 2, width, LANES), jnp.bfloat16),
        scratch_shapes=[pltpu.VMEM(x.shape, x.dtype) for x in operands] + [pltpu.SemaphoreType.DMA((2,))],
        compiler_params=params(chips),
        name="own_rows",
    )(*operands)
    outs = pl.pallas_call(
        other_kernel,
        in_specs=[VMEM] * 4,
        out_specs=[VMEM] * planes + [HBM],
        out_shape=[jax.ShapeDtypeStruct((QUAD, chunk_rows(0)[1], LANES), jnp.bfloat16)] * planes
        + [jax.ShapeDtypeStruct((QUAD, planes, chunk_rows(1)[1], LANES), jnp.bfloat16)],
        scratch_shapes=[
            pltpu.VMEM((QUAD, planes, chunk_rows(1)[1], LANES), jnp.bfloat16),
            pltpu.SemaphoreType.DMA((planes,)),
        ],
        compiler_params=params(chips),
        name="send_rows",
    )(period, other_t, other_sends, own)
    return outs[:planes], outs[planes]


def regroup_kernel(planes, *refs):
    b_ref = refs[1]
    a_refs, a_hbm = refs[2 : planes + 2], refs[planes + 2]
    b_outs, sems = refs[planes + 3 : -1], refs[-1]
    copies = [pltpu.make_async_copy(ref, a_hbm.at[:, j], sems.at[j]) for j, ref in enumerate(a_refs)]
    for copy in copies:
        copy.start()
    for j, out in enumerate(b_outs, 1):
        for q in range(QUAD):
            out[q] = b_ref[q, j]
    for copy in copies:
        copy.wait()


def regroup(after, blocks_a, block_b, chips):
    planes = len(blocks_a)
    outs = pl.pallas_call(
        functools.partial(regroup_kernel, planes),
        in_specs=[VMEM] * (2 + planes),
        out_specs=[HBM] + [VMEM] * (planes - 1),
        out_shape=[jax.ShapeDtypeStruct((QUAD, planes) + blocks_a[0].shape[1:], jnp.bfloat16)]
        + [jax.ShapeDtypeStruct((QUAD,) + block_b.shape[2:], jnp.bfloat16)] * (planes - 1),
        scratch_shapes=[pltpu.SemaphoreType.DMA((planes,))],
        compiler_params=params(chips),
        name="regroup",
    )(after, block_b, *blocks_a)
    return outs[0], outs[1:]


def along_planes(blocks):
    planes = len(blocks) + 1

    def pairs(step):
        return [(2 * p + core, 2 * (p ^ own) + core) for core, own in enumerate((step, turned_step(step))) for p in range(planes)]

    return [lax.ppermute(block, ("plane", "band"), pairs(step)) for step, block in enumerate(blocks, 1)]


def among_cells(array):
    return lax.all_to_all(array, "cell", split_axis=0, concat_axis=0, tiled=True)


def exchange(blocks_a, block_b, chips, after):
    near_b = among_cells(block_b)
    held_a = [blocks_a[0]] + along_planes(blocks_a[1:])
    grouped_a, grouped_b = regroup(after, held_a, near_b, chips)
    return among_cells(grouped_a), [near_b] + along_planes(grouped_b)


def slot_places(slots):
    half = (lax.axis_index("band") ^ (lax.axis_index("cell") & 1)) * HALF
    shift = (QUAD * LANES).bit_length() - 1
    place = slots ^ ((lax.axis_index("plane") << shift) + half)
    turned = (turned_back(place >> shift) << shift) | (place & (QUAD * LANES - 1))
    return jnp.where(lax.axis_index("band") == 0, place, turned)


def blocks_of_first(ref):
    return [ref.at[q, j] for j in range(ref.shape[1]) for q in range(QUAD)]


def blocks_of_second(refs):
    near, far = refs[0], refs[1:]
    return [near.at[q, 0] for q in range(QUAD)] + [ref.at[q] for ref in far for q in range(QUAD)]


def stack_groups(blocks, start, count, table_ref, first, rows):
    per_group = GROUP // LANES
    for c, block in enumerate(blocks):
        g, j = divmod(c, per_group)
        table_ref[pl.ds(g * rows + first, count), j * LANES : (j + 1) * LANES] = block[start : start + count, :]


def index_kernel(after_ref, slots_ref, dwell_ref, addr_ref, building_ref, places_out, dwell_out, addr_out, building_out):
    places_out[...] = slot_places(slots_ref[...])
    dwell_out[...] = f32(dwell_ref[...])
    for ref, out in ((addr_ref, addr_out), (building_ref, building_out)):
        out[...] = jnp.concatenate([ref[c : c + 1, :] for c in range(ref.shape[0])], axis=1)


def make_index(after, tile_slots, dwellings, addr_t, building_t, chips):
    dwell = dwellings.reshape(-1, LANES)
    row = jax.ShapeDtypeStruct((1, addr_t.size), jnp.int32)
    return pl.pallas_call(
        index_kernel,
        in_specs=[HBM] + [VMEM] * 4,
        out_specs=[VMEM] * 4,
        out_shape=[
            jax.ShapeDtypeStruct(tile_slots.shape, jnp.int32),
            jax.ShapeDtypeStruct(dwell.shape, jnp.float32),
            row,
            row,
        ],
        compiler_params=params(chips),
        name="index_rows",
    )(after, tile_slots, dwell, addr_t, building_t)


def gather_columns(table, rows, places):
    found = dot(table, one_hot_groups(places & (GROUP - 1)))
    group = places >> (GROUP.bit_length() - 1)
    out = jnp.zeros((rows, places.shape[1]), jnp.float32)
    for g in range(table.shape[0] // rows):
        out = jnp.where(group == g, found[g * rows : (g + 1) * rows], out)
    return out


def level_kernel(devices, recv_ref, places_ref, absorption_ref, geometry_ref, dwell_ref, addr_ref, *refs):
    level_ref, pay_ref, table = refs
    blocks = blocks_of_first(recv_ref)
    tiles, recv_tile, paths = geometry_ref.shape
    rows = 2 * BANDS
    stack_groups(blocks, blocks[0].shape[0] - rows, rows, table, 0, rows)
    places = places_ref[...]
    per_tile = recv_tile // LANES
    zeros = jnp.zeros((5, paths), jnp.float32)
    for t in range(tiles):
        sums = gather_columns(table[...], rows, places[t : t + 1, :])
        path = jnp.sum(f32(absorption_ref[t]) * (sums[:BANDS] + sums[BANDS:]), axis=0, keepdims=True)
        lhs = bf(jnp.concatenate([*three_parts(path), zeros], axis=0))
        energy = jnp.sum(dot(lhs, geometry_ref[t], NT), axis=0, keepdims=True)
        level = jnp.log(energy) * LOG10_E
        for j in range(per_tile):
            level_ref[t * per_tile + j : t * per_tile + j + 1, :] = level[:, j * LANES : (j + 1) * LANES]

    addr = addr_ref[...]
    cap = addr.shape[1] // devices
    level_rows = level_ref.shape[0]
    parts = [*three_parts(level_ref[...]), dwell_ref[...]]
    found = dot(bf(jnp.concatenate(parts, axis=0)), one_hot_columns(addr & (LANES - 1), LANES))
    row = lax.broadcasted_iota(jnp.int32, (level_rows, addr.shape[1]), 0)
    hit = row == (addr >> (LANES.bit_length() - 1))

    def pick(i):
        part = found[i * level_rows : (i + 1) * level_rows]
        return jnp.sum(jnp.where(hit, part, 0.0), axis=0, keepdims=True)

    dwelt = pick(3)
    weighted = dwelt * ((pick(0) + pick(1)) + pick(2))
    lines = [value[:, c * devices : (c + 1) * devices] for value in (weighted, dwelt) for c in range(cap)]
    square = jnp.concatenate(lines + [jnp.zeros((LANES - 2 * cap, devices), jnp.float32)], axis=0)
    if devices < LANES:
        square = jnp.concatenate([square, jnp.zeros((LANES, LANES - devices), jnp.float32)], axis=1)
    turned = square.T
    for d in range(devices):
        pay_ref[d] = turned[d : d + 1, :]


def make_levels(recv, chips, places, absorption, geometry, dwell, addr):
    tiles, recv_tile, paths = geometry.shape
    devices = 2 * chips
    operands = [recv, places, absorption, geometry, dwell, addr]
    return pl.pallas_call(
        functools.partial(level_kernel, devices),
        in_specs=[VMEM] * len(operands),
        out_specs=[VMEM] * 2,
        out_shape=[
            jax.ShapeDtypeStruct(dwell.shape, jnp.float32),
            jax.ShapeDtypeStruct((devices, 1, LANES), jnp.float32),
        ],
        scratch_shapes=[pltpu.VMEM((chips * LANES // GROUP * 2 * BANDS, GROUP), jnp.bfloat16)],
        compiler_params=params(chips),
        name="levels",
    )(*operands)


def exposure_kernel(planes, *refs):
    places_ref, absorption_ref, geometry_ref, out_hbm, done_ref, table, out_ref, sems = refs[1 + planes :]
    done_ref[...] = jnp.zeros_like(done_ref)
    tiles, recv_tile, paths = geometry_ref.shape
    rows = out_ref.shape[0]
    for (first, last), blocks in zip(CHUNKS, (blocks_of_first(refs[0]), blocks_of_second(refs[1 : 1 + planes]))):
        stack_groups(blocks, 0, (last - first) * HOURS, table, first * HOURS, rows)
    places = places_ref[...]
    copies = []
    for t in range(tiles):
        gathered = gather_columns(table[...], rows, places[t : t + 1, :])
        absorption = f32(absorption_ref[t])
        mixed = jnp.concatenate(
            [absorption[b : b + 1] * gathered[b * HOURS : (b + 1) * HOURS] for b in range(BANDS)], axis=0
        )
        columns = slice(t * recv_tile, (t + 1) * recv_tile)
        out_ref[:, columns] = dot(bf(mixed), geometry_ref[t], NT)
        copy = pltpu.make_async_copy(out_ref.at[:, columns], out_hbm.at[:, columns], sems.at[t])
        copy.start()
        copies.append(copy)
    for copy in copies:
        copy.wait()


def make_exposure(moved, chips, places, absorption, geometry):
    tiles, recv_tile, paths = geometry.shape
    shape = (BANDS * HOURS, tiles * recv_tile)
    operands = [moved[0], *moved[1], places, absorption, geometry]
    return pl.pallas_call(
        functools.partial(exposure_kernel, chips // QUAD),
        in_specs=[VMEM] * len(operands),
        out_specs=[HBM, VMEM],
        out_shape=[jax.ShapeDtypeStruct(shape, jnp.float32), jax.ShapeDtypeStruct((8, LANES), jnp.float32)],
        scratch_shapes=[
            pltpu.VMEM((chips * LANES // GROUP * shape[0], GROUP), jnp.bfloat16),
            pltpu.VMEM(shape, jnp.float32),
            pltpu.SemaphoreType.DMA((tiles,)),
        ],
        compiler_params=params(chips),
        name="exposure",
    )(*operands)


def building_kernel(after_ref, arrived_ref, building_ref, out_ref):
    devices = arrived_ref.shape[0]
    building = building_ref[...]
    cap = building.shape[1] // devices
    square = jnp.concatenate([arrived_ref[s] for s in range(devices)], axis=0)
    if devices < LANES:
        square = jnp.concatenate([square, jnp.zeros((LANES - devices, LANES), jnp.float32)], axis=0)
    turned = square.T

    def line(ref, first):
        return jnp.concatenate([ref[first + c : first + c + 1, :devices] for c in range(cap)], axis=1)

    weighted, dwelt = line(turned, 0), line(turned, cap)
    rows = out_ref.shape[0]
    row = lax.broadcasted_iota(jnp.int32, (rows, building.shape[1]), 0)
    hit = row == (building >> (LANES.bit_length() - 1))
    parts = [jnp.where(hit, value, 0.0) for value in three_parts(weighted) + (dwelt,)]
    table = one_hot_columns(building & (LANES - 1), LANES)
    sums = dot(bf(jnp.concatenate(parts, axis=0)), table, NT)
    numer = (sums[:rows] + sums[rows : 2 * rows]) + sums[2 * rows : 3 * rows]
    out_ref[...] = numer / jnp.maximum(sums[3 * rows :], 1.0)


def make_buildings(after, arrived, building, chips):
    return pl.pallas_call(
        building_kernel,
        in_specs=[VMEM] * 3,
        out_specs=VMEM,
        out_shape=jax.ShapeDtypeStruct((BLD_DEV // LANES, LANES), jnp.float32),
        compiler_params=params(chips),
        name="buildings",
    )(after, arrived, building)


def local(
    emission,
    path_sends,
    tile_slots,
    geometry,
    absorption,
    hour_period,
    dwellings,
    addr_sends,
    addr_building,
    chips,
):
    swap = [(0, 1), (1, 0)]
    emission_t = emission.T
    sends = path_sends[0]
    other_t = lax.ppermute(emission_t, "band", swap)
    other_sends = lax.ppermute(sends, "band", swap)
    period = lax.ppermute(hour_period.reshape(1, HOURS), "band", swap)
    blocks_a, block_b = make_sends(period, emission_t, other_t, sends, other_sends, chips)
    places, dwell, addr, building = make_index(
        blocks_a[0], tile_slots, dwellings, addr_sends[0].T, addr_building[0].T, chips
    )
    moved = exchange(blocks_a, block_b, chips, places)
    levels, pay = make_levels(moved[0], chips, places, absorption, geometry, dwell, addr)
    arrived = lax.all_to_all(pay, AXES, split_axis=0, concat_axis=0, tiled=True)
    exposure_t, done = make_exposure(moved, chips, places, absorption, geometry)
    buildings = make_buildings(done, arrived, building, chips)
    return (levels.reshape(-1), buildings.reshape(-1), exposure_t.T)


def solution(mesh):
    chips = mesh.shape["region"]
    cells = jax.sharding.Mesh(mesh.devices.reshape(chips // QUAD, QUAD, mesh.shape["band"]), AXES)
    in_specs = (
        P(AXES, None),
        P(AXES, None, None),
        P(AXES, None),
        P(AXES, None, None),
        P(AXES, None, None),
        P(),
        P(AXES),
        P(AXES, None, None),
        P(AXES, None, None),
    )
    out_specs = (P(AXES), P(AXES), P(AXES, None))
    body = functools.partial(local, chips=chips)
    return jax.shard_map(body, mesh=cells, in_specs=in_specs, out_specs=out_specs, check_vma=False)
```

```python
import functools

import jax
import jax.numpy as jnp
from jax import lax
from jax.experimental import pallas as pl
from jax.experimental.pallas import tpu as pltpu
from jax.sharding import PartitionSpec as P

HOURS = 24
BANDS = 8
BLD_DEV = 2048
LANES = 128
HALF = LANES // 2
GROUP = 256
AXES = ("plane", "cell", "band")

A_WEIGHTING_DB = [-26.2, -16.1, -8.6, -3.2, 0.0, 1.2, 1.0, -1.1]
GAIN = [1.0, 10.0**0.5, 10.0]
LOG10_E = 0.4342944819032518

QUAD = 4
CHUNKS = ((0, 2), (2, 8))

NT = (((1,), (1,)), ((), ()))
VMEM = pl.BlockSpec(memory_space=pltpu.VMEM)
HBM = pl.BlockSpec(memory_space=pltpu.HBM)


def params(chips):
    return pltpu.CompilerParams(vmem_limit_bytes=min(16 * max(chips // 16, 1), 48) * 1024 * 1024)


def bf(x):
    return x.astype(jnp.bfloat16)


def f32(x):
    return x.astype(jnp.float32)


def three_parts(x):
    hi = f32(bf(x))
    rest = x - hi
    mid = f32(bf(rest))
    return hi, mid, rest - mid


def dot(a, b, dims=(((1,), (0,)), ((), ()))):
    return lax.dot_general(a, b, dims, preferred_element_type=jnp.float32)


def one_hot_columns(index, extent):
    rows = lax.broadcasted_iota(jnp.int32, (extent, index.shape[1]), 0)
    return bf(jnp.where(rows == index, jnp.float32(1.0), jnp.float32(0.0)))


def one_hot_groups(index):
    step = 16
    shape = (step, index.shape[1])
    rows = lax.broadcasted_iota(jnp.int32, shape, 0).astype(jnp.int16)
    wanted = jnp.broadcast_to(index, shape).astype(jnp.int16)
    one, zero = jnp.ones(shape, jnp.bfloat16), jnp.zeros(shape, jnp.bfloat16)
    return jnp.concatenate(
        [jnp.where(wanted == rows + jnp.int16(start), one, zero) for start in range(0, GROUP, step)], axis=0
    )


def merge(low, high):
    lane = lax.broadcasted_iota(jnp.int32, low.shape, 1)
    return jnp.where(lane < HALF, low, high)


def hour_gains(period_row):
    gain = jnp.where(period_row == 0, GAIN[0], jnp.where(period_row == 1, GAIN[1], jnp.where(period_row == 2, GAIN[2], 0.0)))
    shape = (HOURS, HOURS)
    same = lax.broadcasted_iota(jnp.int32, shape, 0) == lax.broadcasted_iota(jnp.int32, shape, 1)
    return jnp.sum(jnp.where(same, jnp.broadcast_to(gain, shape), 0.0), axis=1, keepdims=True)


def band_sums(emission, gains):
    sums = []
    for b in range(BANDS):
        rows = f32(emission[b * HOURS : (b + 1) * HOURS, :])
        factor = 10.0 ** (A_WEIGHTING_DB[b] / 10.0) / HOURS
        sums.append(jnp.sum(rows * (gains * factor), axis=0, keepdims=True))
    total = jnp.concatenate(sums, axis=0)
    high = f32(bf(total))
    return bf(jnp.concatenate([high, total - high], axis=0))


def chunk_rows(i):
    first, last = CHUNKS[i]
    if i == 0:
        return 0, last * HOURS + 2 * BANDS
    return first * HOURS + 2 * BANDS, (last - first) * HOURS


def extend_order(emission, sums):
    cut = CHUNKS[0][1] * HOURS
    return jnp.concatenate([emission[:cut], sums, emission[cut:]], axis=0)


def turned_step(step):
    low, high = step & 1, (step >> 1) & 1
    return (step & ~3) | (((low ^ high) << 1) | high)


def turned_back(step):
    low, high = step & 1, (step >> 1) & 1
    return (step & ~3) | ((low << 1) | (low ^ high))


def lists_of(list_ref, step, swapped):
    plane = lax.axis_index("plane") ^ jnp.where(lax.axis_index("band") == 0, turned_step(step), turned_back(step))
    band = lax.axis_index("band")
    order = [q ^ 1 if swapped else q for q in range(QUAD)]
    return jnp.concatenate([list_ref[pl.ds(2 * (plane * QUAD + q) + band, 1), :] for q in order], axis=1)


def own_kernel(period_hbm, emission_hbm, list_hbm, out_ref, period_ref, emission_ref, list_ref, sems):
    pairs = ((list_hbm, list_ref), (period_hbm, period_ref), (emission_hbm, emission_ref))
    copies = [pltpu.make_async_copy(src, dst, sems.at[i]) for i, (src, dst) in enumerate(pairs)]
    for copy in copies:
        copy.start()
    for copy in copies:
        copy.wait()
    emission = emission_ref[...]
    rows = extend_order(emission, band_sums(emission, hour_gains(period_ref[...])))
    for step in range(out_ref.shape[0]):
        found = bf(dot(rows, one_hot_columns(lists_of(list_ref, step, False), rows.shape[1])))
        for pair in range(QUAD // 2):
            out_ref[step, pair] = found[:, pair * LANES : (pair + 1) * LANES]


def other_kernel(period_ref, emission_ref, list_ref, own_ref, *refs):
    planes = own_ref.shape[0]
    a_refs, (b_hbm, b_ref, sems) = refs[:planes], refs[planes:]
    emission = emission_ref[...]
    rows = extend_order(emission, band_sums(emission, hour_gains(period_ref[...])))
    (start_a, count_a), (start_b, count_b) = chunk_rows(0), chunk_rows(1)
    copies = []
    for step in range(planes):
        found = bf(dot(rows, one_hot_columns(lists_of(list_ref, step, True), rows.shape[1])))
        for pair in range(QUAD // 2):
            other = found[:, pair * LANES : (pair + 1) * LANES]
            own = own_ref[step, pair]
            for odd, block in ((0, merge(own, other)), (1, merge(other, own))):
                q = 2 * pair + odd
                a_refs[step][q] = block[start_a : start_a + count_a]
                b_ref[q, step] = block[start_b : start_b + count_b]
        copy = pltpu.make_async_copy(b_ref.at[:, step], b_hbm.at[:, step], sems.at[step])
        copy.start()
        copies.append(copy)
    for copy in copies:
        copy.wait()


def make_sends(hour_period, emission_t, other_t, sends, other_sends, chips):
    width, segs = emission_t.shape
    total = width + 2 * BANDS
    planes = chips // QUAD
    period = hour_period.reshape(1, HOURS)
    operands = [period, emission_t, sends]
    own = pl.pallas_call(
        own_kernel,
        in_specs=[HBM] * 3,
        out_specs=VMEM,
        out_shape=jax.ShapeDtypeStruct((planes, QUAD // 2, total, LANES), jnp.bfloat16),
        scratch_shapes=[pltpu.VMEM(x.shape, x.dtype) for x in operands] + [pltpu.SemaphoreType.DMA((3,))],
        compiler_params=params(chips),
        name="own_rows",
    )(*operands)
    outs = pl.pallas_call(
        other_kernel,
        in_specs=[VMEM] * 4,
        out_specs=[VMEM] * planes + [HBM],
        out_shape=[jax.ShapeDtypeStruct((QUAD, chunk_rows(0)[1], LANES), jnp.bfloat16)] * planes
        + [jax.ShapeDtypeStruct((QUAD, planes, chunk_rows(1)[1], LANES), jnp.bfloat16)],
        scratch_shapes=[
            pltpu.VMEM((QUAD, planes, chunk_rows(1)[1], LANES), jnp.bfloat16),
            pltpu.SemaphoreType.DMA((planes,)),
        ],
        compiler_params=params(chips),
        name="send_rows",
    )(period, other_t, other_sends, own)
    return outs[:planes], outs[planes]


def regroup_kernel(planes, *refs):
    b_ref, a_refs = refs[1], refs[2 : planes + 2]
    a_outs, b_outs = refs[planes + 2 : planes + 2 + QUAD], refs[planes + 2 + QUAD :]
    cell = lax.axis_index("cell")
    for i, out in enumerate(a_outs):
        for j, ref in enumerate(a_refs):
            out[j] = ref[cell ^ i]
    for j, out in enumerate(b_outs, 1):
        for q in range(QUAD):
            out[q] = b_ref[q, j]


def last_kernel(after_ref, b_ref, out_ref):
    for q in range(QUAD):
        out_ref[q] = b_ref[q, b_ref.shape[1] - 1]


def last_blocks(after, block_b, chips):
    return pl.pallas_call(
        last_kernel,
        in_specs=[VMEM] * 2,
        out_specs=VMEM,
        out_shape=jax.ShapeDtypeStruct((QUAD,) + block_b.shape[2:], jnp.bfloat16),
        compiler_params=params(chips),
        name="last_blocks",
    )(after, block_b)


def regroup(after, blocks_a, block_b, chips):
    planes = len(blocks_a)
    outs = pl.pallas_call(
        functools.partial(regroup_kernel, planes),
        in_specs=[VMEM] * (2 + planes),
        out_specs=[VMEM] * (QUAD + planes - 2),
        out_shape=[jax.ShapeDtypeStruct((planes,) + blocks_a[0].shape[1:], jnp.bfloat16)] * QUAD
        + [jax.ShapeDtypeStruct((QUAD,) + block_b.shape[2:], jnp.bfloat16)] * (planes - 2),
        compiler_params=params(chips),
        name="regroup",
    )(after, block_b, *blocks_a)
    return outs[:QUAD], outs[QUAD:]


def along_plane(block, step, planes):
    pairs = [
        (2 * p + core, 2 * (p ^ own) + core)
        for core, own in enumerate((turned_step(step), turned_back(step)))
        for p in range(planes)
    ]
    return lax.ppermute(block, ("plane", "band"), pairs)


def among_cells(array):
    return lax.all_to_all(array, "cell", split_axis=0, concat_axis=0, tiled=True)


def to_cells(blocks):
    return [blocks[0]] + [
        lax.ppermute(blocks[i], "cell", [(q, q ^ i) for q in range(QUAD)]) for i in range(1, QUAD)
    ]


def exchange(blocks_a, block_b, chips, after):
    planes = len(blocks_a)
    near_b = among_cells(block_b)
    held_a = [blocks_a[0]] + [along_plane(blocks_a[step], step, planes) for step in range(1, planes)]
    grouped_a, grouped_b = regroup(after, held_a, near_b, chips)
    far_b = [along_plane(block, step, planes) for step, block in enumerate(grouped_b, 1)]
    return to_cells(grouped_a), [near_b] + far_b


def slot_places(slots):
    half = (lax.axis_index("band") ^ (lax.axis_index("cell") & 1)) * HALF
    shift = (QUAD * LANES).bit_length() - 1
    place = slots ^ ((lax.axis_index("plane") << shift) + half)
    step = place >> shift
    step = jnp.where(lax.axis_index("band") == 0, turned_back(step), turned_step(step))
    return (step << shift) | (place & (QUAD * LANES - 1))


def blocks_of_second(refs):
    near, far = refs[0], refs[1:]
    return [near.at[q, 0] for q in range(QUAD)] + [ref.at[q] for ref in far for q in range(QUAD)]


def stack_groups(blocks, start, count, table_ref, first, rows):
    per_group = GROUP // LANES
    for c, block in enumerate(blocks):
        g, j = divmod(c, per_group)
        table_ref[pl.ds(g * rows + first, count), j * LANES : (j + 1) * LANES] = block[start : start + count, :]


def stack_steps(arrays, start, count, table_ref, first, rows):
    cell = lax.axis_index("cell")
    per_group = GROUP // LANES
    for i, array in enumerate(arrays):
        for j in range(array.shape[0]):
            place = j * QUAD + (cell ^ i)
            row = pl.multiple_of((place // per_group) * rows + first, 2 * BANDS)
            lane = pl.multiple_of((place % per_group) * LANES, LANES)
            table_ref[pl.ds(row, count), pl.ds(lane, LANES)] = array[j, start : start + count, :]


def index_kernel(after_ref, slots_ref, dwell_ref, addr_ref, building_ref, places_out, dwell_out, addr_out, building_out):
    places_out[...] = slot_places(slots_ref[...])
    dwell_out[...] = f32(dwell_ref[...])
    for ref, out in ((addr_ref, addr_out), (building_ref, building_out)):
        out[...] = jnp.concatenate([ref[c : c + 1, :] for c in range(ref.shape[0])], axis=1)


def make_index(after, tile_slots, dwellings, addr_t, building_t, chips):
    dwell = dwellings.reshape(-1, LANES)
    row = jax.ShapeDtypeStruct((1, addr_t.size), jnp.int32)
    return pl.pallas_call(
        index_kernel,
        in_specs=[HBM] + [VMEM] * 4,
        out_specs=[VMEM] * 4,
        out_shape=[
            jax.ShapeDtypeStruct(tile_slots.shape, jnp.int32),
            jax.ShapeDtypeStruct(dwell.shape, jnp.float32),
            row,
            row,
        ],
        compiler_params=params(chips),
        name="index_rows",
    )(after, tile_slots, dwell, addr_t, building_t)


def gather_columns(table, rows, places):
    found = dot(table, one_hot_groups(places & (GROUP - 1)))
    group = places >> (GROUP.bit_length() - 1)
    out = jnp.zeros((rows, places.shape[1]), jnp.float32)
    for g in range(table.shape[0] // rows):
        out = jnp.where(group == g, found[g * rows : (g + 1) * rows], out)
    return out


def level_kernel(devices, *refs):
    places_ref, absorption_ref, geometry_ref, dwell_ref, addr_ref, level_ref, pay_ref, done_ref, table = refs[QUAD:]
    done_ref[...] = jnp.zeros_like(done_ref)
    tiles, recv_tile, paths = geometry_ref.shape
    rows = 2 * BANDS
    stack_steps(refs[:QUAD], refs[0].shape[1] - rows, rows, table, 0, rows)
    places = places_ref[...]
    per_tile = recv_tile // LANES
    zeros = jnp.zeros((5, paths), jnp.float32)
    for t in range(tiles):
        sums = gather_columns(table[...], rows, places[t : t + 1, :])
        path = jnp.sum(f32(absorption_ref[t]) * (sums[:BANDS] + sums[BANDS:]), axis=0, keepdims=True)
        lhs = bf(jnp.concatenate([*three_parts(path), zeros], axis=0))
        energy = jnp.sum(dot(lhs, geometry_ref[t], NT), axis=0, keepdims=True)
        level = jnp.log(energy) * LOG10_E
        for j in range(per_tile):
            level_ref[t * per_tile + j : t * per_tile + j + 1, :] = level[:, j * LANES : (j + 1) * LANES]

    addr = addr_ref[...]
    cap = addr.shape[1] // devices
    level_rows = level_ref.shape[0]
    parts = [*three_parts(level_ref[...]), dwell_ref[...]]
    found = dot(bf(jnp.concatenate(parts, axis=0)), one_hot_columns(addr & (LANES - 1), LANES))
    row = lax.broadcasted_iota(jnp.int32, (level_rows, addr.shape[1]), 0)
    hit = row == (addr >> (LANES.bit_length() - 1))

    def pick(i):
        part = found[i * level_rows : (i + 1) * level_rows]
        return jnp.sum(jnp.where(hit, part, 0.0), axis=0, keepdims=True)

    dwelt = pick(3)
    weighted = dwelt * ((pick(0) + pick(1)) + pick(2))
    lines = [value[:, c * devices : (c + 1) * devices] for value in (weighted, dwelt) for c in range(cap)]
    square = jnp.concatenate(lines + [jnp.zeros((LANES - 2 * cap, devices), jnp.float32)], axis=0)
    if devices < LANES:
        square = jnp.concatenate([square, jnp.zeros((LANES, LANES - devices), jnp.float32)], axis=1)
    turned = square.T
    for d in range(devices):
        pay_ref[d] = turned[d : d + 1, :]


def make_levels(recv, chips, places, absorption, geometry, dwell, addr):
    tiles, recv_tile, paths = geometry.shape
    devices = 2 * chips
    operands = [*recv, places, absorption, geometry, dwell, addr]
    return pl.pallas_call(
        functools.partial(level_kernel, devices),
        in_specs=[VMEM] * len(operands),
        out_specs=[VMEM] * 3,
        out_shape=[
            jax.ShapeDtypeStruct(dwell.shape, jnp.float32),
            jax.ShapeDtypeStruct((devices, 1, LANES), jnp.float32),
            jax.ShapeDtypeStruct((8, LANES), jnp.float32),
        ],
        scratch_shapes=[pltpu.VMEM((chips * LANES // GROUP * 2 * BANDS, GROUP), jnp.bfloat16)],
        compiler_params=params(chips),
        name="levels",
    )(*operands)


def exposure_kernel(planes, *refs):
    places_ref, absorption_ref, geometry_ref, out_hbm, done_ref, table, out_ref, sems = refs[QUAD + planes :]
    done_ref[...] = jnp.zeros_like(done_ref)
    tiles, recv_tile, paths = geometry_ref.shape
    rows = out_ref.shape[0]
    (first_a, last_a), (first_b, last_b) = CHUNKS
    stack_steps(refs[:QUAD], 0, (last_a - first_a) * HOURS, table, first_a * HOURS, rows)
    stack_groups(blocks_of_second(refs[QUAD : QUAD + planes]), 0, (last_b - first_b) * HOURS, table, first_b * HOURS, rows)
    places = places_ref[...]
    copies = []
    for t in range(tiles):
        gathered = gather_columns(table[...], rows, places[t : t + 1, :])
        absorption = f32(absorption_ref[t])
        mixed = jnp.concatenate(
            [absorption[b : b + 1] * gathered[b * HOURS : (b + 1) * HOURS] for b in range(BANDS)], axis=0
        )
        columns = slice(t * recv_tile, (t + 1) * recv_tile)
        out_ref[:, columns] = dot(bf(mixed), geometry_ref[t], NT)
        copy = pltpu.make_async_copy(out_ref.at[:, columns], out_hbm.at[:, columns], sems.at[t])
        copy.start()
        copies.append(copy)
    for copy in copies:
        copy.wait()


def make_exposure(moved, chips, places, absorption, geometry):
    tiles, recv_tile, paths = geometry.shape
    shape = (BANDS * HOURS, tiles * recv_tile)
    operands = [*moved[0], *moved[1], places, absorption, geometry]
    return pl.pallas_call(
        functools.partial(exposure_kernel, chips // QUAD),
        in_specs=[VMEM] * len(operands),
        out_specs=[HBM, VMEM],
        out_shape=[jax.ShapeDtypeStruct(shape, jnp.float32), jax.ShapeDtypeStruct((8, LANES), jnp.float32)],
        scratch_shapes=[
            pltpu.VMEM((chips * LANES // GROUP * shape[0], GROUP), jnp.bfloat16),
            pltpu.VMEM(shape, jnp.float32),
            pltpu.SemaphoreType.DMA((tiles,)),
        ],
        compiler_params=params(chips),
        name="exposure",
    )(*operands)


def building_kernel(after_ref, arrived_ref, building_ref, out_ref):
    devices = arrived_ref.shape[0]
    building = building_ref[...]
    cap = building.shape[1] // devices
    square = jnp.concatenate([arrived_ref[s] for s in range(devices)], axis=0)
    if devices < LANES:
        square = jnp.concatenate([square, jnp.zeros((LANES - devices, LANES), jnp.float32)], axis=0)
    turned = square.T

    def line(ref, first):
        return jnp.concatenate([ref[first + c : first + c + 1, :devices] for c in range(cap)], axis=1)

    weighted, dwelt = line(turned, 0), line(turned, cap)
    rows = out_ref.shape[0]
    row = lax.broadcasted_iota(jnp.int32, (rows, building.shape[1]), 0)
    hit = row == (building >> (LANES.bit_length() - 1))
    parts = [jnp.where(hit, value, 0.0) for value in three_parts(weighted) + (dwelt,)]
    table = one_hot_columns(building & (LANES - 1), LANES)
    sums = dot(bf(jnp.concatenate(parts, axis=0)), table, NT)
    numer = (sums[:rows] + sums[rows : 2 * rows]) + sums[2 * rows : 3 * rows]
    out_ref[...] = numer / jnp.maximum(sums[3 * rows :], 1.0)


def make_buildings(after, arrived, building, chips):
    return pl.pallas_call(
        building_kernel,
        in_specs=[VMEM] * 3,
        out_specs=VMEM,
        out_shape=jax.ShapeDtypeStruct((BLD_DEV // LANES, LANES), jnp.float32),
        compiler_params=params(chips),
        name="buildings",
    )(after, arrived, building)


def local(
    emission,
    path_sends,
    tile_slots,
    geometry,
    absorption,
    hour_period,
    dwellings,
    addr_sends,
    addr_building,
    chips,
):
    swap = [(0, 1), (1, 0)]
    emission_t = emission.T
    sends = path_sends[0]
    other_t = lax.ppermute(emission_t, "band", swap)
    other_sends = lax.ppermute(sends, "band", swap)
    blocks_a, block_b = make_sends(hour_period, emission_t, other_t, sends, other_sends, chips)
    places, dwell, addr, building = make_index(
        blocks_a[0], tile_slots, dwellings, addr_sends[0].T, addr_building[0].T, chips
    )
    moved = exchange(blocks_a, block_b, chips, places)
    levels, pay, ready = make_levels(moved[0], chips, places, absorption, geometry, dwell, addr)
    planes = chips // QUAD
    moved[1].append(along_plane(last_blocks(ready, moved[1][0], chips), planes - 1, planes))
    arrived = lax.all_to_all(pay, AXES, split_axis=0, concat_axis=0, tiled=True)
    exposure_t, done = make_exposure(moved, chips, places, absorption, geometry)
    buildings = make_buildings(done, arrived, building, chips)
    return (levels.reshape(-1), buildings.reshape(-1), exposure_t.T)


def solution(mesh):
    chips = mesh.shape["region"]
    cells = jax.sharding.Mesh(mesh.devices.reshape(chips // QUAD, QUAD, mesh.shape["band"]), AXES)
    in_specs = (
        P(AXES, None),
        P(AXES, None, None),
        P(AXES, None),
        P(AXES, None, None),
        P(AXES, None, None),
        P(),
        P(AXES),
        P(AXES, None, None),
        P(AXES, None, None),
    )
    out_specs = (P(AXES), P(AXES), P(AXES, None))
    body = functools.partial(local, chips=chips)
    return jax.shard_map(body, mesh=cells, in_specs=in_specs, out_specs=out_specs, check_vma=False)
```

```python
import functools

import jax
import jax.numpy as jnp
from jax import lax
from jax.experimental import pallas as pl
from jax.experimental.pallas import tpu as pltpu
from jax.sharding import PartitionSpec as P

HOURS = 24
BANDS = 8
BLD_DEV = 2048
LANES = 128
HALF = LANES // 2
GROUP = 256
AXES = ("plane", "cell", "band")

A_WEIGHTING_DB = [-26.2, -16.1, -8.6, -3.2, 0.0, 1.2, 1.0, -1.1]
GAIN = [1.0, 10.0**0.5, 10.0]
LOG10_E = 0.4342944819032518

QUAD = 4
CHUNKS = ((0, 2), (2, 8))

NT = (((1,), (1,)), ((), ()))
VMEM = pl.BlockSpec(memory_space=pltpu.VMEM)
HBM = pl.BlockSpec(memory_space=pltpu.HBM)


def params(chips):
    return pltpu.CompilerParams(vmem_limit_bytes=min(16 * max(chips // 16, 1), 48) * 1024 * 1024)


def bf(x):
    return x.astype(jnp.bfloat16)


def f32(x):
    return x.astype(jnp.float32)


def three_parts(x):
    hi = f32(bf(x))
    rest = x - hi
    mid = f32(bf(rest))
    return hi, mid, rest - mid


def dot(a, b, dims=(((1,), (0,)), ((), ()))):
    return lax.dot_general(a, b, dims, preferred_element_type=jnp.float32)


def one_hot_columns(index, extent):
    rows = lax.broadcasted_iota(jnp.int32, (extent, index.shape[1]), 0)
    return bf(jnp.where(rows == index, jnp.float32(1.0), jnp.float32(0.0)))


def one_hot_groups(index):
    step = 16
    shape = (step, index.shape[1])
    rows = lax.broadcasted_iota(jnp.int32, shape, 0).astype(jnp.int16)
    wanted = jnp.broadcast_to(index, shape).astype(jnp.int16)
    one, zero = jnp.ones(shape, jnp.bfloat16), jnp.zeros(shape, jnp.bfloat16)
    return jnp.concatenate(
        [jnp.where(wanted == rows + jnp.int16(start), one, zero) for start in range(0, GROUP, step)], axis=0
    )


def merge(low, high):
    lane = lax.broadcasted_iota(jnp.int32, low.shape, 1)
    return jnp.where(lane < HALF, low, high)


def hour_gains(period_row):
    gain = jnp.where(period_row == 0, GAIN[0], jnp.where(period_row == 1, GAIN[1], jnp.where(period_row == 2, GAIN[2], 0.0)))
    shape = (HOURS, HOURS)
    same = lax.broadcasted_iota(jnp.int32, shape, 0) == lax.broadcasted_iota(jnp.int32, shape, 1)
    return jnp.sum(jnp.where(same, jnp.broadcast_to(gain, shape), 0.0), axis=1, keepdims=True)


def band_sums(emission, gains):
    sums = []
    for b in range(BANDS):
        rows = f32(emission[b * HOURS : (b + 1) * HOURS, :])
        factor = 10.0 ** (A_WEIGHTING_DB[b] / 10.0) / HOURS
        sums.append(jnp.sum(rows * (gains * factor), axis=0, keepdims=True))
    total = jnp.concatenate(sums, axis=0)
    high = f32(bf(total))
    return bf(jnp.concatenate([high, total - high], axis=0))


def chunk_rows(i):
    first, last = CHUNKS[i]
    if i == 0:
        return 0, last * HOURS + 2 * BANDS
    return first * HOURS + 2 * BANDS, (last - first) * HOURS


def extend_order(emission, sums):
    cut = CHUNKS[0][1] * HOURS
    return jnp.concatenate([emission[:cut], sums, emission[cut:]], axis=0)


def turned_step(step):
    low, high = step & 1, (step >> 1) & 1
    return (step & ~3) | (((low ^ high) << 1) | high)


def turned_back(step):
    low, high = step & 1, (step >> 1) & 1
    return (step & ~3) | ((low << 1) | (low ^ high))


def lists_of(list_ref, step, swapped):
    plane = lax.axis_index("plane") ^ jnp.where(lax.axis_index("band") == 0, turned_step(step), turned_back(step))
    band = lax.axis_index("band")
    order = [q ^ 1 if swapped else q for q in range(QUAD)]
    return jnp.concatenate([list_ref[pl.ds(2 * (plane * QUAD + q) + band, 1), :] for q in order], axis=1)


def own_kernel(period_hbm, emission_hbm, list_hbm, out_ref, period_ref, emission_ref, list_ref, sems):
    pairs = ((list_hbm, list_ref), (period_hbm, period_ref), (emission_hbm, emission_ref))
    copies = [pltpu.make_async_copy(src, dst, sems.at[i]) for i, (src, dst) in enumerate(pairs)]
    for copy in copies:
        copy.start()
    for copy in copies:
        copy.wait()
    emission = emission_ref[...]
    rows = extend_order(emission, band_sums(emission, hour_gains(period_ref[...])))
    for step in range(out_ref.shape[0]):
        found = bf(dot(rows, one_hot_columns(lists_of(list_ref, step, False), rows.shape[1])))
        for pair in range(QUAD // 2):
            out_ref[step, pair] = found[:, pair * LANES : (pair + 1) * LANES]


def other_kernel(period_ref, emission_ref, list_ref, own_ref, *refs):
    planes = own_ref.shape[0]
    a_refs, (b_hbm, b_ref, sems) = refs[:planes], refs[planes:]
    emission = emission_ref[...]
    rows = extend_order(emission, band_sums(emission, hour_gains(period_ref[...])))
    (start_a, count_a), (start_b, count_b) = chunk_rows(0), chunk_rows(1)
    copies = []
    for step in range(planes):
        found = bf(dot(rows, one_hot_columns(lists_of(list_ref, step, True), rows.shape[1])))
        for pair in range(QUAD // 2):
            other = found[:, pair * LANES : (pair + 1) * LANES]
            own = own_ref[step, pair]
            for odd, block in ((0, merge(own, other)), (1, merge(other, own))):
                q = 2 * pair + odd
                a_refs[step][q] = block[start_a : start_a + count_a]
                b_ref[q, step] = block[start_b : start_b + count_b]
        copy = pltpu.make_async_copy(b_ref.at[:, step], b_hbm.at[:, step], sems.at[step])
        copy.start()
        copies.append(copy)
    for copy in copies:
        copy.wait()


def make_sends(hour_period, emission_t, other_t, sends, other_sends, chips):
    width, segs = emission_t.shape
    total = width + 2 * BANDS
    planes = chips // QUAD
    period = hour_period.reshape(1, HOURS)
    operands = [period, emission_t, sends]
    own = pl.pallas_call(
        own_kernel,
        in_specs=[HBM] * 3,
        out_specs=VMEM,
        out_shape=jax.ShapeDtypeStruct((planes, QUAD // 2, total, LANES), jnp.bfloat16),
        scratch_shapes=[pltpu.VMEM(x.shape, x.dtype) for x in operands] + [pltpu.SemaphoreType.DMA((3,))],
        compiler_params=params(chips),
        name="own_rows",
    )(*operands)
    outs = pl.pallas_call(
        other_kernel,
        in_specs=[VMEM] * 4,
        out_specs=[VMEM] * planes + [HBM],
        out_shape=[jax.ShapeDtypeStruct((QUAD, chunk_rows(0)[1], LANES), jnp.bfloat16)] * planes
        + [jax.ShapeDtypeStruct((QUAD, planes, chunk_rows(1)[1], LANES), jnp.bfloat16)],
        scratch_shapes=[
            pltpu.VMEM((QUAD, planes, chunk_rows(1)[1], LANES), jnp.bfloat16),
            pltpu.SemaphoreType.DMA((planes,)),
        ],
        compiler_params=params(chips),
        name="send_rows",
    )(period, other_t, other_sends, own)
    return outs[:planes], outs[planes]


def regroup_kernel(planes, *refs):
    b_ref, a_refs = refs[1], refs[2 : planes + 2]
    a_outs, b_outs = refs[planes + 2 : planes + 2 + QUAD], refs[planes + 2 + QUAD :]
    cell = lax.axis_index("cell")
    for i, out in enumerate(a_outs):
        for j, ref in enumerate(a_refs):
            out[j] = ref[cell ^ i]
    for j, out in enumerate(b_outs, 1):
        for q in range(QUAD):
            out[q] = b_ref[q, j]


def last_kernel(after_ref, b_ref, out_ref):
    for q in range(QUAD):
        out_ref[q] = b_ref[q, b_ref.shape[1] - 1]


def last_blocks(after, block_b, chips):
    return pl.pallas_call(
        last_kernel,
        in_specs=[VMEM] * 2,
        out_specs=VMEM,
        out_shape=jax.ShapeDtypeStruct((QUAD,) + block_b.shape[2:], jnp.bfloat16),
        compiler_params=params(chips),
        name="last_blocks",
    )(after, block_b)


def regroup(after, blocks_a, block_b, chips):
    planes = len(blocks_a)
    outs = pl.pallas_call(
        functools.partial(regroup_kernel, planes),
        in_specs=[VMEM] * (2 + planes),
        out_specs=[VMEM] * (QUAD + planes - 2),
        out_shape=[jax.ShapeDtypeStruct((planes,) + blocks_a[0].shape[1:], jnp.bfloat16)] * QUAD
        + [jax.ShapeDtypeStruct((QUAD,) + block_b.shape[2:], jnp.bfloat16)] * (planes - 2),
        compiler_params=params(chips),
        name="regroup",
    )(after, block_b, *blocks_a)
    return outs[:QUAD], outs[QUAD:]


def along_plane(block, step, planes):
    pairs = [
        (2 * p + core, 2 * (p ^ own) + core)
        for core, own in enumerate((turned_step(step), turned_back(step)))
        for p in range(planes)
    ]
    return lax.ppermute(block, ("plane", "band"), pairs)


def among_cells(array):
    return lax.all_to_all(array, "cell", split_axis=0, concat_axis=0, tiled=True)


def to_cells(blocks):
    return [blocks[0]] + [
        lax.ppermute(blocks[i], "cell", [(q, q ^ i) for q in range(QUAD)]) for i in range(1, QUAD)
    ]


def exchange(blocks_a, block_b, chips, after):
    planes = len(blocks_a)
    near_b = among_cells(block_b)
    held_a = [blocks_a[0]] + [along_plane(blocks_a[step], step, planes) for step in range(1, planes)]
    grouped_a, grouped_b = regroup(after, held_a, near_b, chips)
    far_b = [along_plane(block, step, planes) for step, block in enumerate(grouped_b, 1)]
    return to_cells(grouped_a), [near_b] + far_b


def slot_places(slots):
    half = (lax.axis_index("band") ^ (lax.axis_index("cell") & 1)) * HALF
    shift = (QUAD * LANES).bit_length() - 1
    place = slots ^ ((lax.axis_index("plane") << shift) + half)
    step = place >> shift
    step = jnp.where(lax.axis_index("band") == 0, turned_back(step), turned_step(step))
    return (step << shift) | (place & (QUAD * LANES - 1))


def blocks_of_second(refs):
    near, far = refs[0], refs[1:]
    return [near.at[q, 0] for q in range(QUAD)] + [ref.at[q] for ref in far for q in range(QUAD)]


def stack_groups(blocks, start, count, table_ref, first, rows, skip=0):
    per_group = GROUP // LANES
    for c, block in enumerate(blocks[skip:], skip):
        g, j = divmod(c, per_group)
        table_ref[pl.ds(g * rows + first, count), j * LANES : (j + 1) * LANES] = block[start : start + count, :]


def stack_steps(arrays, start, count, table_ref, first, rows):
    cell = lax.axis_index("cell")
    per_group = GROUP // LANES
    for i, array in enumerate(arrays):
        for j in range(array.shape[0]):
            place = j * QUAD + (cell ^ i)
            row = pl.multiple_of((place // per_group) * rows + first, 2 * BANDS)
            lane = pl.multiple_of((place % per_group) * LANES, LANES)
            table_ref[pl.ds(row, count), pl.ds(lane, LANES)] = array[j, start : start + count, :]


def index_kernel(after_ref, slots_ref, dwell_ref, addr_ref, building_ref, places_out, dwell_out, addr_out, building_out):
    places_out[...] = slot_places(slots_ref[...])
    dwell_out[...] = f32(dwell_ref[...])
    for ref, out in ((addr_ref, addr_out), (building_ref, building_out)):
        out[...] = jnp.concatenate([ref[c : c + 1, :] for c in range(ref.shape[0])], axis=1)


def make_index(after, tile_slots, dwellings, addr_t, building_t, chips):
    dwell = dwellings.reshape(-1, LANES)
    row = jax.ShapeDtypeStruct((1, addr_t.size), jnp.int32)
    return pl.pallas_call(
        index_kernel,
        in_specs=[HBM] + [VMEM] * 4,
        out_specs=[VMEM] * 4,
        out_shape=[
            jax.ShapeDtypeStruct(tile_slots.shape, jnp.int32),
            jax.ShapeDtypeStruct(dwell.shape, jnp.float32),
            row,
            row,
        ],
        compiler_params=params(chips),
        name="index_rows",
    )(after, tile_slots, dwell, addr_t, building_t)


def gather_columns(table, rows, places):
    found = dot(table, one_hot_groups(places & (GROUP - 1)))
    group = places >> (GROUP.bit_length() - 1)
    out = jnp.zeros((rows, places.shape[1]), jnp.float32)
    for g in range(table.shape[0] // rows):
        out = jnp.where(group == g, found[g * rows : (g + 1) * rows], out)
    return out


def level_kernel(devices, *refs):
    places_ref, absorption_ref, geometry_ref, dwell_ref, addr_ref, level_ref, pay_ref, done_ref, table = refs[QUAD:]
    done_ref[...] = jnp.zeros_like(done_ref)
    tiles, recv_tile, paths = geometry_ref.shape
    rows = 2 * BANDS
    stack_steps(refs[:QUAD], refs[0].shape[1] - rows, rows, table, 0, rows)
    places = places_ref[...]
    per_tile = recv_tile // LANES
    zeros = jnp.zeros((5, paths), jnp.float32)
    for t in range(tiles):
        sums = gather_columns(table[...], rows, places[t : t + 1, :])
        path = jnp.sum(f32(absorption_ref[t]) * (sums[:BANDS] + sums[BANDS:]), axis=0, keepdims=True)
        lhs = bf(jnp.concatenate([*three_parts(path), zeros], axis=0))
        energy = jnp.sum(dot(lhs, geometry_ref[t], NT), axis=0, keepdims=True)
        level = jnp.log(energy) * LOG10_E
        for j in range(per_tile):
            level_ref[t * per_tile + j : t * per_tile + j + 1, :] = level[:, j * LANES : (j + 1) * LANES]

    addr = addr_ref[...]
    cap = addr.shape[1] // devices
    level_rows = level_ref.shape[0]
    parts = [*three_parts(level_ref[...]), dwell_ref[...]]
    found = dot(bf(jnp.concatenate(parts, axis=0)), one_hot_columns(addr & (LANES - 1), LANES))
    row = lax.broadcasted_iota(jnp.int32, (level_rows, addr.shape[1]), 0)
    hit = row == (addr >> (LANES.bit_length() - 1))

    def pick(i):
        part = found[i * level_rows : (i + 1) * level_rows]
        return jnp.sum(jnp.where(hit, part, 0.0), axis=0, keepdims=True)

    dwelt = pick(3)
    weighted = dwelt * ((pick(0) + pick(1)) + pick(2))
    lines = [value[:, c * devices : (c + 1) * devices] for value in (weighted, dwelt) for c in range(cap)]
    square = jnp.concatenate(lines + [jnp.zeros((LANES - 2 * cap, devices), jnp.float32)], axis=0)
    if devices < LANES:
        square = jnp.concatenate([square, jnp.zeros((LANES, LANES - devices), jnp.float32)], axis=1)
    turned = square.T
    for d in range(devices):
        pay_ref[d] = turned[d : d + 1, :]


def make_levels(recv, chips, places, absorption, geometry, dwell, addr):
    tiles, recv_tile, paths = geometry.shape
    devices = 2 * chips
    operands = [*recv, places, absorption, geometry, dwell, addr]
    return pl.pallas_call(
        functools.partial(level_kernel, devices),
        in_specs=[VMEM] * len(operands),
        out_specs=[VMEM] * 3,
        out_shape=[
            jax.ShapeDtypeStruct(dwell.shape, jnp.float32),
            jax.ShapeDtypeStruct((devices, 1, LANES), jnp.float32),
            jax.ShapeDtypeStruct((8, LANES), jnp.float32),
        ],
        scratch_shapes=[pltpu.VMEM((chips * LANES // GROUP * 2 * BANDS, GROUP), jnp.bfloat16)],
        compiler_params=params(chips),
        name="levels",
    )(*operands)


def exposure_kernel(planes, *refs):
    places_ref, absorption_ref, geometry_ref, out_hbm, done_ref, table, out_ref, sems, last_ref, last_sem = refs[QUAD + planes :]
    fetch = pltpu.make_async_copy(refs[QUAD + planes - 1], last_ref, last_sem)
    fetch.start()
    done_ref[...] = jnp.zeros_like(done_ref)
    tiles, recv_tile, paths = geometry_ref.shape
    rows = out_ref.shape[0]
    (first_a, last_a), (first_b, last_b) = CHUNKS
    stack_steps(refs[:QUAD], 0, (last_a - first_a) * HOURS, table, first_a * HOURS, rows)
    blocks = blocks_of_second([*refs[QUAD : QUAD + planes - 1], last_ref])
    count = (last_b - first_b) * HOURS
    stack_groups(blocks[:-QUAD], 0, count, table, first_b * HOURS, rows)
    fetch.wait()
    stack_groups(blocks, 0, count, table, first_b * HOURS, rows, skip=len(blocks) - QUAD)
    places = places_ref[...]
    copies = []
    for t in range(tiles):
        gathered = gather_columns(table[...], rows, places[t : t + 1, :])
        absorption = f32(absorption_ref[t])
        mixed = jnp.concatenate(
            [absorption[b : b + 1] * gathered[b * HOURS : (b + 1) * HOURS] for b in range(BANDS)], axis=0
        )
        columns = slice(t * recv_tile, (t + 1) * recv_tile)
        out_ref[:, columns] = dot(bf(mixed), geometry_ref[t], NT)
        copy = pltpu.make_async_copy(out_ref.at[:, columns], out_hbm.at[:, columns], sems.at[t])
        copy.start()
        copies.append(copy)
    for copy in copies:
        copy.wait()


def make_exposure(moved, chips, places, absorption, geometry):
    tiles, recv_tile, paths = geometry.shape
    shape = (BANDS * HOURS, tiles * recv_tile)
    operands = [*moved[0], *moved[1], places, absorption, geometry]
    return pl.pallas_call(
        functools.partial(exposure_kernel, chips // QUAD),
        in_specs=[VMEM] * (len(operands) - 4) + [HBM] + [VMEM] * 3,
        out_specs=[HBM, VMEM],
        out_shape=[jax.ShapeDtypeStruct(shape, jnp.float32), jax.ShapeDtypeStruct((8, LANES), jnp.float32)],
        scratch_shapes=[
            pltpu.VMEM((chips * LANES // GROUP * shape[0], GROUP), jnp.bfloat16),
            pltpu.VMEM(shape, jnp.float32),
            pltpu.SemaphoreType.DMA((tiles,)),
            pltpu.VMEM(moved[1][-1].shape, jnp.bfloat16),
            pltpu.SemaphoreType.DMA,
        ],
        compiler_params=params(chips),
        name="exposure",
    )(*operands)


def building_kernel(after_ref, arrived_ref, building_ref, out_ref):
    devices = arrived_ref.shape[0]
    building = building_ref[...]
    cap = building.shape[1] // devices
    square = jnp.concatenate([arrived_ref[s] for s in range(devices)], axis=0)
    if devices < LANES:
        square = jnp.concatenate([square, jnp.zeros((LANES - devices, LANES), jnp.float32)], axis=0)
    turned = square.T

    def line(ref, first):
        return jnp.concatenate([ref[first + c : first + c + 1, :devices] for c in range(cap)], axis=1)

    weighted, dwelt = line(turned, 0), line(turned, cap)
    rows = out_ref.shape[0]
    row = lax.broadcasted_iota(jnp.int32, (rows, building.shape[1]), 0)
    hit = row == (building >> (LANES.bit_length() - 1))
    parts = [jnp.where(hit, value, 0.0) for value in three_parts(weighted) + (dwelt,)]
    table = one_hot_columns(building & (LANES - 1), LANES)
    sums = dot(bf(jnp.concatenate(parts, axis=0)), table, NT)
    numer = (sums[:rows] + sums[rows : 2 * rows]) + sums[2 * rows : 3 * rows]
    out_ref[...] = numer / jnp.maximum(sums[3 * rows :], 1.0)


def make_buildings(after, arrived, building, chips):
    return pl.pallas_call(
        building_kernel,
        in_specs=[VMEM] * 3,
        out_specs=VMEM,
        out_shape=jax.ShapeDtypeStruct((BLD_DEV // LANES, LANES), jnp.float32),
        compiler_params=params(chips),
        name="buildings",
    )(after, arrived, building)


def local(
    emission,
    path_sends,
    tile_slots,
    geometry,
    absorption,
    hour_period,
    dwellings,
    addr_sends,
    addr_building,
    chips,
):
    swap = [(0, 1), (1, 0)]
    emission_t = emission.T
    sends = path_sends[0]
    other_t = lax.ppermute(emission_t, "band", swap)
    other_sends = lax.ppermute(sends, "band", swap)
    blocks_a, block_b = make_sends(hour_period, emission_t, other_t, sends, other_sends, chips)
    places, dwell, addr, building = make_index(
        blocks_a[0], tile_slots, dwellings, addr_sends[0].T, addr_building[0].T, chips
    )
    moved = exchange(blocks_a, block_b, chips, places)
    levels, pay, ready = make_levels(moved[0], chips, places, absorption, geometry, dwell, addr)
    planes = chips // QUAD
    moved[1].append(along_plane(last_blocks(ready, moved[1][0], chips), planes - 1, planes))
    arrived = lax.all_to_all(pay, AXES, split_axis=0, concat_axis=0, tiled=True)
    exposure_t, done = make_exposure(moved, chips, places, absorption, geometry)
    buildings = make_buildings(done, arrived, building, chips)
    return (levels.reshape(-1), buildings.reshape(-1), exposure_t.T)


def solution(mesh):
    chips = mesh.shape["region"]
    cells = jax.sharding.Mesh(mesh.devices.reshape(chips // QUAD, QUAD, mesh.shape["band"]), AXES)
    in_specs = (
        P(AXES, None),
        P(AXES, None, None),
        P(AXES, None),
        P(AXES, None, None),
        P(AXES, None, None),
        P(),
        P(AXES),
        P(AXES, None, None),
        P(AXES, None, None),
    )
    out_specs = (P(AXES), P(AXES), P(AXES, None))
    body = functools.partial(local, chips=chips)
    return jax.shard_map(body, mesh=cells, in_specs=in_specs, out_specs=out_specs, check_vma=False)
```
